32 devices in a mesh: dp: 2 (over core), row: 4 (over y, x), col: 4 (over z).
Axes of the slice: x: 2, y: 2, z: 4, core: 2. Of those that a mesh axis runs over, the one named last changes fastest.
Arguments:
- tokens: bfloat16 [2, 4608, 4096], P('dp', 'col', 'row'), may hold values from -6 to 6
- kept_index: int32 [2, 2048], P('dp'), may hold values from 0 to 4095, as said below
- w_query: bfloat16 [4608, 4096], P(('dp', 'row'), 'col'), may hold values from -0.125 to 0.125
- cotangent: bfloat16 [2, 4096, 2048], P('dp', 'col', 'row'), may hold values from -6 to 6
Outputs:
- queries: bfloat16 [2, 4096, 2048], P('dp', 'col', 'row')
- grad_kept: float32 [2, 4608, 2048], P('dp', 'col', 'row')
- grad_weight: float32 [4608, 4096], P(('dp', 'row'), 'col')
The draws below stay inside these ranges and needn't reach their ends.
Inputs may be any that keep to these rules, and one draw needn't show every extreme that they name: `kept_index`: in each sequence the positions increase strictly. For every block b of 1024 positions (positions b * 1024 to (b + 1) * 1024 - 1), the number of kept positions before the block lies between b * 512 and b * 512 + 128; the upper end is reached in every sequence.
All inputs are finite; a program needn't handle non-finite values.
Results may differ from the reference program's by a relative error of at most 0.001.
Values may be sent and summed in bfloat16 or wider, within the bound.
No kernel may reach another device: no remote copies, remote signals or barrier semaphores. Data moves between devices by JAX's collectives and lax.ppermute only.
A program may use at most 128 MiB of HBM per device.

```python
import jax
import jax.numpy as jnp

D = 4608
HEADS = 32
HEAD = 128
SEQ_DEV = 1024
KEEP_DEV = 512
DRIFT = 128
SEQ = 4096
KEEP = 2048
SEQS = 2
N_ROW = 4


def draw_kept_index(key, part):

    def one_sequence(seq_key):
        pair_key, force_key, place_key = jax.random.split(seq_key, 3)
        pair_count = N_ROW // 2
        surplus = jax.random.randint(pair_key, (pair_count,), 0, DRIFT + 1)
        forced = jax.random.randint(force_key, (), 0, pair_count)
        surplus = jnp.where(jnp.arange(pair_count) == forced, DRIFT, surplus)
        counts = jnp.stack([KEEP_DEV + surplus, KEEP_DEV - surplus], axis=1).reshape(N_ROW)
        starts = jnp.cumsum(counts) - counts
        block_keys = jax.random.split(place_key, N_ROW)
        ranks = jax.vmap(lambda block_key: jax.random.permutation(block_key, SEQ_DEV))(block_keys)
        chosen = ranks < counts[:, None]
        order = jnp.cumsum(chosen.astype(jnp.int32), axis=1) - 1
        target = jnp.where(chosen, starts[:, None] + order, KEEP).astype(jnp.int32)
        positions = (jnp.arange(N_ROW)[:, None] * SEQ_DEV + jnp.arange(SEQ_DEV)[None, :]).astype(jnp.int32)
        empty = jnp.zeros((KEEP,), jnp.int32)
        return empty.at[target.reshape(-1)].set(positions.reshape(-1), mode='drop')
    seq_keys = jax.random.split(key, SEQS)
    return jax.vmap(one_sequence)(seq_keys)


def spiked(drawn, own_key, source, target, parts, factor):
    def block_of(dim):
        return (jnp.arange(drawn.shape[dim]) // (drawn.shape[dim] // parts)).reshape((-1,) + (1,) * (drawn.ndim - 1 - dim))

    first = jax.random.permutation(own_key, parts)[block_of(target)]
    far = (block_of(target) + parts // 2) % parts
    return jnp.where((block_of(source) == first) | (block_of(source) == far), factor * drawn, drawn)


def level_of(rng, extent, shards, smallest, largest):
    loudness, own = 1.0, jax.random.fold_in(rng, 6)
    for position, blocks in shards:
        heights = jnp.exp(jax.random.uniform(jax.random.fold_in(own, position), (blocks,), jnp.float32, smallest / len(shards), largest / len(shards)))
        loudness = loudness * jnp.repeat(heights, extent[position] // blocks).reshape([-1 if axis == position else 1 for axis in range(len(extent))])
    return loudness


def scatter_about(rng, dims, width, reach, cuts=(), kind=jnp.bfloat16):
    values = jax.random.normal(rng, dims, jnp.float32) * width
    if len(cuts) > 0:
        values = level_of(rng, dims, cuts, -0.22, 0.18) * values
    return jnp.clip(values, min=-reach, max=reach).astype(kind)


def noise_with(stream_key, extent, scale, reach, cuts, heavy, dtype=jnp.bfloat16):
    drawn = scale * jax.random.normal(stream_key, extent, jnp.float32)
    if cuts:
        drawn = drawn * level_of(stream_key, extent, cuts, -0.22, 0.18)
    return jnp.clip(spiked(drawn, jax.random.fold_in(stream_key, 3), *heavy), -reach, reach).astype(dtype)


def setup_inputs(seed: int = 0) -> dict:
    arg_keys = jax.random.split(jax.random.key(seed), 5)
    return {
        "tokens": noise_with(arg_keys[0], (SEQS, D, SEQ), 1.0, 6.0, ((0, 2), (1, 4), (2, 4)), (2, 1, 4, 2.0)),
        "kept_index": draw_kept_index(jax.random.fold_in(arg_keys[4], 71), 0),
        "w_query": noise_with(arg_keys[2], (D, HEADS * HEAD), D ** -0.5, 0.125, ((0, 8), (1, 4)), (1, 0, 8, 2.0)),
        "cotangent": scatter_about(arg_keys[3], (SEQS, HEADS * HEAD, KEEP), 1.0, 6.0, ((0, 2), (1, 4), (2, 4))),
    }


def reference(tokens, kept_index, w_query, cotangent):
    queries_list = []
    grads_list = []
    grad_weight = jnp.zeros((w_query.shape[0], w_query.shape[1]), jnp.float32)
    for seq_number in range(SEQS):
        kept_x = jnp.take(tokens[seq_number], kept_index[seq_number], axis=1)
        queries_list.append(jnp.dot(w_query.T, kept_x, preferred_element_type=jnp.float32).astype(jnp.bfloat16))
        grads_list.append(jnp.dot(w_query, cotangent[seq_number], preferred_element_type=jnp.float32))
        grad_weight = grad_weight + jnp.dot(kept_x, cotangent[seq_number].T, preferred_element_type=jnp.float32)
    return jnp.stack(queries_list), jnp.stack(grads_list), grad_weight
```

```python
import jax
import jax.numpy as jnp
from jax import lax
from jax.sharding import PartitionSpec as P

HEADER = 16
OFFSET = 512.0
F32 = jnp.float32
F16 = jnp.float16


def mm(a, b, ca, cb):
    return lax.dot_general(a, b, (((ca,), (cb,)), ((), ())), preferred_element_type=F32)


def exponent(bound):
    return jnp.clip(jnp.floor(14.99 - jnp.log2(jnp.maximum(bound, 1e-30))), -100.0, 100.0)


def encode(values, expo):
    rows, cols = values.shape
    padded = jnp.pad(values, ((0, HEADER), (0, 0))) * jnp.exp2(expo)
    row = lax.broadcasted_iota(jnp.int32, (rows + HEADER, cols), 0)
    return jnp.where(row < rows, padded, expo + OFFSET).astype(F16)


def header(payload):
    code = payload[-1, 0].astype(F32)
    return code > 0.0, jnp.where(code > 0.0, code - OFFSET, 0.0)


def decode(payload):
    _, expo = header(payload)
    return payload[:-HEADER].astype(F32) * jnp.exp2(-expo)


def amax(values):
    return jnp.max(jnp.abs(values)).astype(F32)


def per_device(tokens, kept_index, w_query, cotangent):
    n_dp, n_row, n_col = (lax.axis_size(a) for a in ("dp", "row", "col"))
    dp, row, col = (lax.axis_index(a) for a in ("dp", "row", "col"))
    seq_x = tokens[0]
    cot = cotangent[0]
    d_dev, seq_dev = seq_x.shape
    w_rows = w_query.shape[0]
    keep_dev = cot.shape[1]
    heads = cot.shape[0]
    drift = keep_dev // 4
    parts = 2 if w_rows % 32 == 0 else 1
    sub = w_rows // parts
    blocks = d_dev // w_rows
    shard = blocks * sub
    half = (n_col // n_dp) * shard

    w_parts = [
        lax.all_gather(w_query[p * sub : (p + 1) * sub], ("dp", "row"), axis=0, tiled=True)
        for p in range(parts)
    ]

    block_base = row * seq_dev
    own_keep = lax.dynamic_slice_in_dim(kept_index[0], row * keep_dev, keep_dev)
    next_keep = lax.dynamic_slice_in_dim(kept_index[0], (row + 1) * keep_dev, drift)
    position_ids = jnp.arange(seq_dev, dtype=jnp.int32)
    onehot_own = (position_ids[:, None] == (own_keep - block_base)[None, :]).astype(jnp.bfloat16)
    onehot_send = (position_ids[:, None] == (next_keep - block_base)[None, :]).astype(jnp.bfloat16)
    leaving = mm(seq_x, onehot_send, 1, 0).astype(jnp.bfloat16)
    arrived = lax.ppermute(leaving, "row", [(r, r + 1) for r in range(n_row - 1)])
    own_part = mm(seq_x, onehot_own, 1, 0)
    padded = jnp.pad(arrived.astype(F32), ((0, 0), (0, keep_dev - drift)))
    kept = (own_part + padded).astype(jnp.bfloat16).reshape(blocks, parts, sub, keep_dev)

    def along(value, sources, step):
        return lax.ppermute(value, "col", [(c, c + step) for c in sources])

    panels = []
    for p in range(parts):
        own = kept[:, p].reshape(shard, keep_dev)
        from_left, from_right = [own], [own]
        for t in range(1, n_col):
            from_left.append(along(from_left[-1], range(t - 1, n_col - 1), 1))
            from_right.append(along(from_right[-1], range(1, n_col - t + 1), -1))
        line = jnp.concatenate(from_left[:0:-1] + [own] + from_right[1:], axis=0)
        panels.append(lax.dynamic_slice_in_dim(line, (n_col - 1 - col) * shard, n_col * shard))

    grads = []
    for p in range(parts):
        partial = mm(w_parts[p], cot, 1, 0)
        bound = amax(partial)

        def block_of(index):
            return lax.dynamic_slice_in_dim(partial, jnp.clip(index, 0, n_col - 1) * shard, shard)

        def one_way(step):
            payload = None
            for t in range(1, n_col):
                place = col if step > 0 else n_col - 1 - col
                target = n_col - t + place
                target = target if step > 0 else n_col - 1 - target
                value = block_of(target)
                total = bound
                if payload is not None:
                    came, expo = header(payload)
                    total = total + jnp.where(came, jnp.exp2(15.0 - expo), 0.0)
                    value = value + decode(payload)
                sources = range(t) if step > 0 else range(n_col - 1, n_col - 1 - t, -1)
                payload = along(encode(value, exponent(total)), sources, step)
            return decode(payload)

        grads.append(block_of(col) + (one_way(1) + one_way(-1)))
    grad_kept = jnp.stack([g.reshape(blocks, sub, keep_dev) for g in grads], axis=1)
    grad_kept = grad_kept.reshape(d_dev, keep_dev)

    swap = [(i, i ^ 1) for i in range(n_dp)]
    cot_other = lax.ppermute(cot, "dp", swap)
    weight_rows = []
    for p in range(parts):
        mine = lax.dynamic_slice_in_dim(panels[p], dp * half, half)
        give = lax.dynamic_slice_in_dim(panels[p], (n_dp - 1 - dp) * half, half)
        other = lax.ppermute(give, "dp", swap)
        partial = mm(mine, cot, 1, 1) + mm(other, cot_other, 1, 1)
        expo = exponent(amax(partial))
        total = lax.dynamic_slice_in_dim(partial, row * sub, sub)
        came = []
        for step in range(1, n_row):
            piece = lax.dynamic_slice_in_dim(partial, (row ^ step) * sub, sub)
            came.append(
                lax.ppermute(encode(piece, expo), "row", [(r, r ^ step) for r in range(n_row)])
            )
        for payload in came:
            total = total + decode(payload)
        weight_rows.append(total)
    grad_weight = jnp.concatenate(weight_rows, axis=0)

    queries = sum(mm(w_parts[p], panels[p], 0, 0) for p in range(parts))
    return (queries.astype(jnp.bfloat16)[None], grad_kept[None], grad_weight)


def solution(mesh):
    in_specs = (
        P("dp", "col", "row"),
        P("dp", None),
        P(("dp", "row"), "col"),
        P("dp", "col", "row"),
    )
    out_specs = (P("dp", "col", "row"), P("dp", "col", "row"), P(("dp", "row"), "col"))
    return jax.shard_map(
        per_device, mesh=mesh, in_specs=in_specs, out_specs=out_specs, check_vma=False
    )
```

```python
import functools

import jax
import jax.numpy as jnp
from jax import lax
from jax.experimental import pallas as pl
from jax.experimental.pallas import tpu as pltpu
from jax.sharding import PartitionSpec as P

HEADER = 16
OFFSET = 128.0
F32 = jnp.float32
BF16 = jnp.bfloat16
MIB = 1 << 20
ANY = pl.BlockSpec(memory_space=pl.ANY)
VMEM = pl.BlockSpec(memory_space=pltpu.VMEM)
SMEM = pl.BlockSpec(memory_space=pltpu.SMEM)


def shape(dims, dtype):
    return jax.ShapeDtypeStruct(dims, dtype)


def params(mib):
    return pltpu.CompilerParams(vmem_limit_bytes=mib * MIB)


def cost(flops, moved):
    return pl.CostEstimate(flops=int(flops), bytes_accessed=int(moved), transcendentals=0)


def dot(a, b, ca, cb):
    return lax.dot_general(a, b, (((ca,), (cb,)), ((), ())), preferred_element_type=F32)


def exponent(bound):
    return jnp.clip(jnp.floor(14.99 - jnp.log2(jnp.maximum(bound, 1e-30))), -100.0, 100.0)


def power(values, scale):
    v = values * scale
    square = v * v
    fourth = square * square
    return (fourth * square * (v * jnp.abs(v))).astype(BF16)


def root(code, scale):
    y = code.astype(F32)
    quarter = lax.rsqrt(lax.rsqrt(jnp.maximum(jnp.abs(y), 1e-37)))
    size = quarter * lax.rsqrt(quarter) * scale
    return jnp.where(y > 0.0, size, jnp.where(y < 0.0, -size, 0.0))


def tile_max(values):
    most = jnp.max(jnp.abs(values), axis=0, keepdims=True)
    return jnp.broadcast_to(jnp.max(most, axis=1, keepdims=True), (8, 128))


def write_payload(out_ref, values, bound):
    rows = out_ref.shape[0] - HEADER
    expo = exponent(bound)
    out_ref[:rows, :] = power(values, jnp.exp2(expo)[0:1, 0:1])
    code = jnp.broadcast_to((expo + OFFSET)[0:1, 0:1], (HEADER, out_ref.shape[1]))
    out_ref[rows:, :] = code.astype(BF16)


def read_header(rows):
    code = rows[0:8, 0:128].astype(F32)
    came = code > 0.0
    expo = jnp.where(came, code - OFFSET, 0.0)
    return jnp.exp2(-expo), jnp.where(came, jnp.exp2(15.0 - expo), 0.0)


def pick_kernel(index_ref, x_ref, out_ref):
    onehot = lax.broadcasted_iota(jnp.int32, (x_ref.shape[1], index_ref.shape[1]), 0) == index_ref[...]
    out_ref[...] = dot(x_ref[...], onehot.astype(F32).astype(BF16), 1, 0).astype(BF16)


def pick_parts_kernel(blocks, sub, index_ref, x_ref, dep_ref, *out_refs):
    onehot = lax.broadcasted_iota(jnp.int32, (x_ref.shape[1], index_ref.shape[1]), 0) == index_ref[...]
    onehot = onehot.astype(F32).astype(BF16)
    parts = len(out_refs)
    for b in range(blocks):
        for p, out_ref in enumerate(out_refs):
            rows = x_ref[pl.ds((b * parts + p) * sub, sub), :]
            out_ref[pl.ds(b * sub, sub), :] = dot(rows, onehot, 1, 0).astype(BF16)


def add_arrived_kernel(blocks, sub, parts, arrived_ref, *refs):
    in_refs, out_refs = refs[:parts], refs[parts:]
    for b in range(blocks):
        for p in range(parts):
            rows = pl.ds(b * sub, sub)
            came = arrived_ref[pl.ds((b * parts + p) * sub, sub), :]
            out_refs[p][rows, :] = in_refs[p][rows, :] + came


def kept_tokens(seq_x, own, leaving_index, blocks, parts, sub, row_pairs):
    d_dev, seq_dev = seq_x.shape
    keep_dev, drift = own.shape[1], leaving_index.shape[1]
    leaving = pl.pallas_call(
        pick_kernel,
        out_shape=shape((d_dev, drift), BF16),
        in_specs=[VMEM, VMEM],
        out_specs=VMEM,
        compiler_params=params(32),
        cost_estimate=cost(2 * d_dev * seq_dev * drift, 2 * d_dev * seq_dev),
        name="pick_leaving",
    )(leaving_index, seq_x)
    arrived = lax.ppermute(leaving, "row", row_pairs)
    picked = pl.pallas_call(
        functools.partial(pick_parts_kernel, blocks, sub),
        out_shape=[shape((blocks * sub, keep_dev), BF16)] * parts,
        in_specs=[VMEM, VMEM, ANY],
        out_specs=[VMEM] * parts,
        compiler_params=params(32),
        cost_estimate=cost(2 * d_dev * seq_dev * keep_dev, 2 * d_dev * seq_dev),
        name="pick_own",
    )(own, seq_x, leaving)
    window = pl.BlockSpec((blocks * sub, drift), lambda i: (0, 0))
    kept = pl.pallas_call(
        functools.partial(add_arrived_kernel, blocks, sub, parts),
        grid=(1,),
        out_shape=[shape((blocks * sub, keep_dev), BF16)] * parts,
        in_specs=[pl.BlockSpec((d_dev, drift), lambda i: (0, 0))] + [window] * parts,
        out_specs=[window] * parts,
        input_output_aliases={1 + p: p for p in range(parts)},
        compiler_params=params(16),
        cost_estimate=cost(0, 6 * d_dev * drift),
        name="add_arrived",
    )(arrived, *picked)
    return kept, leaving


def split_kernel(sub, dep_ref, w_ref, *refs):
    out_refs, sem = refs[:-1], refs[-1]
    copies = [
        pltpu.make_async_copy(w_ref.at[pl.ds(p * sub, sub), :], out_ref, sem.at[p])
        for p, out_ref in enumerate(out_refs)
    ]
    for copy in copies:
        copy.start()
    for copy in copies:
        copy.wait()


def split_rows(array, parts, dep):
    if parts == 1:
        return [array]
    sub = array.shape[0] // parts
    return pl.pallas_call(
        functools.partial(split_kernel, sub),
        out_shape=[shape((sub, array.shape[1]), array.dtype)] * parts,
        in_specs=[ANY, ANY],
        out_specs=[ANY] * parts,
        scratch_shapes=[pltpu.SemaphoreType.DMA((parts,))],
        cost_estimate=cost(0, 4 * array.size),
        name="split_rows",
    )(dep, array)


def partial_kernel(w_ref, cot_ref, dep_ref, out_ref, bound_ref, right_ref, left_ref):
    value = dot(w_ref[...], cot_ref[...], 1, 0)
    out_ref[...] = value
    bound = tile_max(value)
    bound_ref[...] = bound

    @pl.when(pl.program_id(0) == 0)
    def _():
        write_payload(left_ref, value, bound)

    @pl.when(pl.program_id(0) == pl.num_programs(0) - 1)
    def _():
        write_payload(right_ref, value, bound)


def first_sums(w_part, cot, n_col, dep):
    rows, heads = w_part.shape
    shard = rows // n_col
    keep = cot.shape[1]
    payload = pl.BlockSpec((shard + HEADER, keep), lambda i: (0, 0))
    return pl.pallas_call(
        partial_kernel,
        grid=(n_col,),
        out_shape=[
            shape((rows, keep), F32),
            shape((n_col * 8, 128), F32),
            shape((shard + HEADER, keep), BF16),
            shape((shard + HEADER, keep), BF16),
        ],
        in_specs=[
            pl.BlockSpec((shard, heads), lambda i: (i, 0)),
            pl.BlockSpec((heads, keep), lambda i: (0, 0)),
            ANY,
        ],
        out_specs=[
            pl.BlockSpec((shard, keep), lambda i: (i, 0)),
            pl.BlockSpec((8, 128), lambda i: (i, 0)),
            payload,
            payload,
        ],
        compiler_params=params(32),
        cost_estimate=cost(2 * rows * heads * keep, 2 * rows * heads + 4 * rows * keep),
        name="grad_kept_partial",
    )(w_part, cot, dep)


def pass_on_kernel(at_ref, g_r, b_r, came_r, g_l, b_l, came_l, dep_ref, out_r, out_l):
    for g, b, came, out in ((g_r, b_r, came_r, out_r), (g_l, b_l, came_l, out_l)):
        rows = came.shape[0] - HEADER
        undo, bound = read_header(came[rows:, :])
        value = g[...] + root(came[:rows, :], undo[0:1, 0:1])
        write_payload(out, value, b[...] + bound)


def pass_on(at, sums, bounds, came_r, came_l, dep):
    shard = came_r.shape[0] - HEADER
    keep = came_r.shape[1]
    whole = pl.BlockSpec((shard + HEADER, keep), lambda i, at: (0, 0))

    def own(n):
        return [
            pl.BlockSpec((shard, keep), lambda i, at: (at[n], 0)),
            pl.BlockSpec((8, 128), lambda i, at: (at[n], 0)),
        ]

    return pl.pallas_call(
        pass_on_kernel,
        grid_spec=pltpu.PrefetchScalarGridSpec(
            num_scalar_prefetch=1,
            grid=(1,),
            in_specs=own(0) + [whole] + own(1) + [whole, ANY],
            out_specs=[whole, whole],
        ),
        out_shape=[shape((shard + HEADER, keep), BF16)] * 2,
        compiler_params=params(24),
        cost_estimate=cost(0, 16 * shard * keep),
        name="grad_kept_pass_on",
    )(at, sums, bounds, came_r, sums, bounds, came_l, dep)


def last_kernel(at_ref, g_ref, r_ref, rh_ref, l_ref, lh_ref, base_ref, out_ref):
    undo_r, _ = read_header(rh_ref[...])
    undo_l, _ = read_header(lh_ref[...])
    total = root(r_ref[...], undo_r[0:1, 0:1]) + root(l_ref[...], undo_l[0:1, 0:1])
    out_ref[0] = g_ref[...] + total


def last_sums(at, sums, came_r, came_l, base, part, parts, blocks):
    shard = came_r.shape[0] - HEADER
    keep = came_r.shape[1]
    sub = shard // blocks
    rows = pl.BlockSpec((sub, keep), lambda b, at: (b, 0))
    head = pl.BlockSpec((HEADER, keep), lambda b, at: (shard // HEADER, 0))
    return pl.pallas_call(
        last_kernel,
        grid_spec=pltpu.PrefetchScalarGridSpec(
            num_scalar_prefetch=1,
            grid=(blocks,),
            in_specs=[
                pl.BlockSpec((sub, keep), lambda b, at: (at[0] * blocks + b, 0)),
                rows,
                head,
                rows,
                head,
                ANY,
            ],
            out_specs=pl.BlockSpec((1, sub, keep), lambda b, at: (b * parts + part, 0, 0)),
        ),
        out_shape=shape((blocks * parts, sub, keep), F32),
        input_output_aliases={6: 0} if part else {},
        compiler_params=params(24),
        cost_estimate=cost(0, 12 * shard * keep),
        name="grad_kept_last",
    )(at, sums, came_r, came_r, came_l, came_l, base)


def fetch(refs, source, target, sem):
    for j, ref in enumerate(refs):

        @pl.when(source == j)
        def _():
            pltpu.make_async_copy(ref, target, sem).start()

    return pltpu.make_async_copy(refs[0], target, sem)


def give_kernel(n_col, n_half, where_ref, *refs):
    sources, (out_ref, sem) = refs[: 2 * n_col - 1], refs[2 * n_col - 1 :]
    other = 1 - where_ref[0]
    shard = sources[0].shape[0]
    waits = [
        fetch(
            sources,
            other * n_half + i - where_ref[2] + n_col - 1,
            out_ref.at[pl.ds(i * shard, shard), :],
            sem.at[i],
        )
        for i in range(n_half)
    ]
    for wait in waits:
        wait.wait()


def other_half(where, line, n_col, n_half):
    shard, keep = line[0].shape
    return pl.pallas_call(
        functools.partial(give_kernel, n_col, n_half),
        out_shape=shape((n_half * shard, keep), BF16),
        in_specs=[SMEM] + [ANY] * len(line),
        out_specs=ANY,
        scratch_shapes=[pltpu.SemaphoreType.DMA((n_half,))],
        cost_estimate=cost(0, 4 * n_half * shard * keep),
        name="half_for_other_core",
    )(where, *line)


def weight_kernel(n_col, n_half, n_row, where_ref, cot_ref, cot_other_ref, other_ref, dep_ref, *refs):
    sources = refs[: 2 * n_col - 1]
    own_ref, send_refs = refs[2 * n_col - 1], refs[2 * n_col : 2 * n_col + n_row - 1]
    mine_ref, total_ref, sem = refs[2 * n_col + n_row - 1 :]
    dp, row, col = where_ref[0], where_ref[1], where_ref[2]
    shard = sources[0].shape[0]
    waits = [
        fetch(
            sources,
            dp * n_half + i - col + n_col - 1,
            mine_ref.at[pl.ds(i * shard, shard), :],
            sem.at[i],
        )
        for i in range(n_half)
    ]
    for wait in waits:
        wait.wait()
    sub = own_ref.shape[0]
    bound = jnp.zeros((8, 128), F32)
    for step in range(n_row):
        rows = pl.ds(pl.multiple_of((row ^ step) * sub, 16), sub)
        value = dot(mine_ref[rows, :], cot_ref[...], 1, 1) + dot(other_ref[rows, :], cot_other_ref[...], 1, 1)
        if step == 0:
            own_ref[...] = value
        else:
            total_ref[step - 1] = value
            bound = jnp.maximum(bound, tile_max(value))
    for step in range(1, n_row):
        write_payload(send_refs[step - 1], total_ref[step - 1], bound)


def weight_partial(where, cot, cot_other, other, line, n_col, n_half, n_row, dep):
    half, keep = other.shape
    heads = cot.shape[0]
    sub = half // n_row
    return pl.pallas_call(
        functools.partial(weight_kernel, n_col, n_half, n_row),
        out_shape=[shape((sub, heads), F32)] + [shape((sub + HEADER, heads), BF16)] * (n_row - 1),
        in_specs=[SMEM, VMEM, VMEM, VMEM, ANY] + [ANY] * len(line),
        out_specs=[VMEM] * n_row,
        scratch_shapes=[
            pltpu.VMEM((half, keep), BF16),
            pltpu.VMEM((n_row - 1, sub, heads), F32),
            pltpu.SemaphoreType.DMA((n_half,)),
        ],
        compiler_params=params(40),
        cost_estimate=cost(4 * half * keep * heads, 4 * half * (keep + heads)),
        name="grad_weight_partial",
    )(where, cot, cot_other, other, dep, *line)


def weight_last_kernel(n_came, *refs):
    own_ref, came_refs, out_ref = refs[0], refs[1 : 1 + n_came], refs[-1]
    rows = own_ref.shape[0]
    total = own_ref[...]
    for came in came_refs:
        undo, _ = read_header(came[rows:, :])
        total = total + root(came[:rows, :], undo[0:1, 0:1])
    out_ref[...] = total


def weight_last(own, came, base, part, parts):
    sub, heads = own.shape
    tile = 256
    rows = pl.BlockSpec((sub, tile), lambda i: (0, i))
    whole = pl.BlockSpec((sub + HEADER, tile), lambda i: (0, i))
    return pl.pallas_call(
        functools.partial(weight_last_kernel, len(came)),
        grid=(heads // tile,),
        out_shape=shape((sub * parts, heads), F32),
        in_specs=[rows] + [whole] * len(came) + [ANY],
        out_specs=pl.BlockSpec((sub, tile), lambda i: (part, i)),
        input_output_aliases={1 + len(came): 0} if part else {},
        compiler_params=params(24),
        cost_estimate=cost(0, 14 * sub * heads),
        name="grad_weight_last",
    )(own, *came, base)


def query_kernel(n_col, parts, where_ref, dep_ref, *refs):
    w_refs = refs[:parts]
    count = 2 * n_col - 1
    lines = [refs[parts + p * count : parts + (p + 1) * count] for p in range(parts)]
    out_ref, panel_ref, sem = refs[parts + parts * count :]
    shard = lines[0][0].shape[0]

    @pl.when(pl.program_id(0) == 0)
    def _():
        waits = [
            fetch(
                lines[p],
                i - where_ref[2] + n_col - 1,
                panel_ref.at[p, pl.ds(i * shard, shard), :],
                sem.at[p, i],
            )
            for p in range(parts)
            for i in range(n_col)
        ]
        for wait in waits:
            wait.wait()

    total = dot(w_refs[0][...], panel_ref[0], 0, 0)
    for p in range(1, parts):
        total = total + dot(w_refs[p][...], panel_ref[p], 0, 0)
    out_ref[...] = total.astype(BF16)


def all_queries(where, w_parts, lines, n_col, dep):
    parts = len(w_parts)
    rows, heads = w_parts[0].shape
    shard, keep = lines[0][0].shape
    tile = 256
    return pl.pallas_call(
        functools.partial(query_kernel, n_col, parts),
        grid=(heads // tile,),
        out_shape=shape((heads, keep), BF16),
        in_specs=[SMEM, ANY]
        + [pl.BlockSpec((rows, tile), lambda i: (0, i))] * parts
        + [ANY] * (len(lines[0]) * parts),
        out_specs=pl.BlockSpec((tile, keep), lambda i: (i, 0)),
        scratch_shapes=[
            pltpu.VMEM((parts, rows, keep), BF16),
            pltpu.SemaphoreType.DMA((parts, n_col)),
        ],
        compiler_params=params(48),
        cost_estimate=cost(2 * parts * rows * heads * keep, 2 * parts * rows * (heads + keep)),
        name="queries",
    )(where, dep, *w_parts, *[piece for line in lines for piece in line])


def per_device(tokens, kept_index, w_query, cotangent):
    n_dp, n_row, n_col = (lax.axis_size(a) for a in ("dp", "row", "col"))
    dp, row, col = (lax.axis_index(a) for a in ("dp", "row", "col"))
    where = jnp.stack([dp, row, col]).astype(jnp.int32)
    seq_x = tokens[0]
    cot = cotangent[0]
    d_dev, seq_dev = seq_x.shape
    w_rows = w_query.shape[0]
    keep_dev = cot.shape[1]
    drift = keep_dev // 4
    parts = 2 if w_rows % 32 == 0 else 1
    sub = w_rows // parts
    blocks = d_dev // w_rows
    n_half = n_col // n_dp

    base = row * seq_dev
    own = lax.dynamic_slice_in_dim(kept_index, row * keep_dev, keep_dev, axis=1) - base
    leaving_index = lax.dynamic_slice_in_dim(kept_index, (row + 1) * keep_dev, drift, axis=1) - base
    row_pairs = [(r, r + 1) for r in range(n_row - 1)]
    kept, leaving = kept_tokens(seq_x, own, leaving_index, blocks, parts, sub, row_pairs)

    w_parts = [
        lax.all_gather(w, ("dp", "row"), axis=0, tiled=True) for w in split_rows(w_query, parts, leaving)
    ]
    swap = [(i, i ^ 1) for i in range(n_dp)]
    cot_other = lax.ppermute(cot, "dp", swap)

    def along(value, sources, step):
        return lax.ppermute(value, "col", [(c, c + step) for c in sources])

    from_left = [[k] for k in kept]
    from_right = [[k] for k in kept]

    def gather_step(p, t):
        from_left[p].append(along(from_left[p][-1], range(t - 1, n_col - 1), 1))
        from_right[p].append(along(from_right[p][-1], range(1, n_col - t + 1), -1))

    def reduce_send(right, left, t):
        return (
            along(right, range(t), 1),
            along(left, range(n_col - 1, n_col - 1 - t, -1), -1),
        )

    for t in range(1, n_col):
        for p in range(parts):
            gather_step(p, t)
    lines = [from_left[p][:0:-1] + [kept[p]] + from_right[p][1:] for p in range(parts)]

    grad_kept = None
    dep = kept[0]
    at_end = col.reshape(1).astype(jnp.int32)
    for p in range(parts):
        sums, bounds, right, left = first_sums(w_parts[p], cot, n_col, dep)
        for t in range(1, n_col):
            if t > 1:
                at = jnp.stack([n_col - t + col, t - 1 - (n_col - 1 - col)])
                at = jnp.clip(at, 0, n_col - 1).astype(jnp.int32)
                right, left = pass_on(at, sums, bounds, right, left, lines[p][n_col - 1 - t + 1])
            right, left = reduce_send(right, left, t)
        if grad_kept is None:
            grad_kept = last_sums(at_end, sums, right, left, dep, p, parts, blocks)
        else:
            grad_kept = last_sums(at_end, sums, right, left, grad_kept, p, parts, blocks)

    grad_weight = dep
    for p in range(parts):
        give = other_half(where, lines[p], n_col, n_half)
        other = lax.ppermute(give, "dp", swap)
        total, *sends = weight_partial(where, cot, cot_other, other, lines[p], n_col, n_half, n_row, dep)
        came = [
            lax.ppermute(send, "row", [(r, r ^ step) for r in range(n_row)])
            for step, send in enumerate(sends, 1)
        ]
        grad_weight = weight_last(total, came, grad_weight, p, parts)

    queries = all_queries(where, w_parts, lines, n_col, total)
    return (queries[None], grad_kept.reshape(1, d_dev, keep_dev), grad_weight)


def solution(mesh):
    in_specs = (
        P("dp", "col", "row"),
        P("dp", None),
        P(("dp", "row"), "col"),
        P("dp", "col", "row"),
    )
    out_specs = (P("dp", "col", "row"), P("dp", "col", "row"), P(("dp", "row"), "col"))
    return jax.shard_map(
        per_device, mesh=mesh, in_specs=in_specs, out_specs=out_specs, check_vma=False
    )
```

```python
import functools

import jax
import jax.numpy as jnp
from jax import lax
from jax.experimental import pallas as pl
from jax.experimental.pallas import tpu as pltpu
from jax.sharding import PartitionSpec as P

HEADER = 16
OFFSET = 128.0
F32 = jnp.float32
BF16 = jnp.bfloat16
MIB = 1 << 20
ANY = pl.BlockSpec(memory_space=pl.ANY)
VMEM = pl.BlockSpec(memory_space=pltpu.VMEM)
SMEM = pl.BlockSpec(memory_space=pltpu.SMEM)


def shape(dims, dtype):
    return jax.ShapeDtypeStruct(dims, dtype)


PARAMS = pltpu.CompilerParams(vmem_limit_bytes=60 * MIB)


def cost(flops, moved):
    return pl.CostEstimate(flops=int(flops), bytes_accessed=int(moved), transcendentals=0)


def dot(a, b, ca, cb):
    return lax.dot_general(a, b, (((ca,), (cb,)), ((), ())), preferred_element_type=F32)


def exponent(bound):
    return jnp.clip(jnp.floor(14.99 - jnp.log2(jnp.maximum(bound, 1e-30))), -100.0, 100.0)


def power(values, scale):
    v = values * scale
    square = v * v
    fourth = square * square
    return (fourth * square * (v * jnp.abs(v))).astype(BF16)


def root(code, scale):
    y = code.astype(F32)
    quarter = lax.rsqrt(lax.rsqrt(jnp.maximum(jnp.abs(y), 1e-37)))
    size = quarter * lax.rsqrt(quarter) * scale
    return jnp.where(y > 0.0, size, jnp.where(y < 0.0, -size, 0.0))


def tile_max(values):
    most = jnp.max(jnp.abs(values), axis=0, keepdims=True)
    return jnp.broadcast_to(jnp.max(most, axis=1, keepdims=True), (8, 128))


def write_payload(out_ref, values, bound):
    rows = out_ref.shape[0] - HEADER
    expo = exponent(bound)
    out_ref[:rows, :] = power(values, jnp.exp2(expo)[0:1, 0:1])
    write_header(out_ref, expo)


def write_header(out_ref, expo):
    rows = out_ref.shape[0] - HEADER
    code = jnp.broadcast_to((expo + OFFSET)[0:1, 0:1], (HEADER, out_ref.shape[1]))
    out_ref[rows:, :] = code.astype(BF16)


def read_header(rows):
    code = rows[0:8, 0:128].astype(F32)
    came = code > 0.0
    expo = jnp.where(came, code - OFFSET, 0.0)
    return jnp.exp2(-expo), jnp.where(came, jnp.exp2(15.0 - expo), 0.0)


def onehot_of(index_ref, first, count, seq_dev):
    row = lax.axis_index("row")
    index = index_ref[:, pl.ds(pl.multiple_of(first, 128), count)] - row * seq_dev
    positions = lax.broadcasted_iota(jnp.int32, (seq_dev, count), 0)
    return (positions == index).astype(F32).astype(BF16)


def pick_kernel(keep_dev, n_row, index_ref, x_ref, out_ref, onehot_ref):
    count = out_ref.shape[1]

    @pl.when(pl.program_id(0) == 0)
    def _():
        after = jnp.minimum(lax.axis_index("row") + 1, n_row - 1) * keep_dev
        onehot_ref[...] = onehot_of(index_ref, after, count, x_ref.shape[1])

    out_ref[...] = dot(x_ref[...], onehot_ref[...], 1, 0).astype(BF16)


def pick_parts_kernel(parts, index_ref, x_ref, dep_ref, *refs):
    out_refs, onehot_ref = refs[:parts], refs[parts]
    i = pl.program_id(0)
    sub, seq_dev = x_ref.shape
    keep_dev = onehot_ref.shape[1]

    @pl.when(i == 0)
    def _():
        onehot_ref[...] = onehot_of(index_ref, lax.axis_index("row") * keep_dev, keep_dev, seq_dev)

    picked = dot(x_ref[...], onehot_ref[...], 1, 0).astype(BF16)
    rows = pl.ds(pl.multiple_of((i // parts) * sub, 16), sub)
    for p, out_ref in enumerate(out_refs):

        @pl.when(i % parts == p)
        def _():
            out_ref[rows, :] = picked


def add_arrived_kernel(blocks, sub, parts, arrived_ref, *refs):
    in_refs, out_refs = refs[:parts], refs[parts:]
    for b in range(blocks):
        for p in range(parts):
            rows = pl.ds(b * sub, sub)
            came = arrived_ref[pl.ds((b * parts + p) * sub, sub), :]
            out_refs[p][rows, :] = in_refs[p][rows, :] + came


def kept_tokens(seq_x, kept_index, keep_dev, drift, blocks, parts, sub, n_row):
    d_dev, seq_dev = seq_x.shape
    index = pl.BlockSpec(kept_index.shape, lambda i: (0, 0))
    rows = pl.BlockSpec((sub, seq_dev), lambda i: (i, 0))
    leaving = pl.pallas_call(
        functools.partial(pick_kernel, keep_dev, n_row),
        grid=(d_dev // sub,),
        out_shape=shape((d_dev, drift), BF16),
        in_specs=[index, rows],
        out_specs=pl.BlockSpec((sub, drift), lambda i: (i, 0)),
        scratch_shapes=[pltpu.VMEM((seq_dev, drift), BF16)],
        compiler_params=PARAMS,
        cost_estimate=cost(2 * d_dev * seq_dev * drift, 2 * d_dev * seq_dev),
        name="pick_leaving",
    )(kept_index, seq_x)
    arrived = lax.ppermute(leaving, "row", [(r, r + 1) for r in range(n_row - 1)])
    picked = pl.pallas_call(
        functools.partial(pick_parts_kernel, parts),
        grid=(d_dev // sub,),
        out_shape=[shape((blocks * sub, keep_dev), BF16)] * parts,
        in_specs=[index, rows, ANY],
        out_specs=[pl.BlockSpec((blocks * sub, keep_dev), lambda i: (0, 0))] * parts,
        scratch_shapes=[pltpu.VMEM((seq_dev, keep_dev), BF16)],
        compiler_params=PARAMS,
        cost_estimate=cost(2 * d_dev * seq_dev * keep_dev, 2 * d_dev * seq_dev),
        name="pick_own",
    )(kept_index, seq_x, leaving)
    window = pl.BlockSpec((blocks * sub, drift), lambda i: (0, 0))
    kept = pl.pallas_call(
        functools.partial(add_arrived_kernel, blocks, sub, parts),
        grid=(1,),
        out_shape=[shape((blocks * sub, keep_dev), BF16)] * parts,
        in_specs=[pl.BlockSpec((d_dev, drift), lambda i: (0, 0))] + [window] * parts,
        out_specs=[window] * parts,
        input_output_aliases={1 + p: p for p in range(parts)},
        compiler_params=PARAMS,
        cost_estimate=cost(0, 6 * d_dev * drift),
        name="add_arrived",
    )(arrived, *picked)
    return kept, leaving


def split_kernel(sub, dep_ref, w_ref, *refs):
    out_refs, sem = refs[:-1], refs[-1]
    copies = [
        pltpu.make_async_copy(w_ref.at[pl.ds(p * sub, sub), :], out_ref, sem.at[p])
        for p, out_ref in enumerate(out_refs)
    ]
    for copy in copies:
        copy.start()
    for copy in copies:
        copy.wait()


def split_rows(array, parts, dep):
    if parts == 1:
        return [array]
    sub = array.shape[0] // parts
    return pl.pallas_call(
        functools.partial(split_kernel, sub),
        out_shape=[shape((sub, array.shape[1]), array.dtype)] * parts,
        in_specs=[ANY, ANY],
        out_specs=[VMEM] * parts,
        scratch_shapes=[pltpu.SemaphoreType.DMA((parts,))],
        compiler_params=PARAMS,
        cost_estimate=cost(0, 4 * array.size),
        name="split_rows",
    )(dep, array)


def partial_kernel(w_ref, cot_ref, dep_ref, out_ref, bound_ref, right_ref, left_ref):
    value = dot(w_ref[...], cot_ref[...], 1, 0)
    out_ref[...] = value
    bound = tile_max(value)
    bound_ref[...] = bound

    @pl.when(pl.program_id(0) == 0)
    def _():
        write_payload(left_ref, value, bound)

    @pl.when(pl.program_id(0) == pl.num_programs(0) - 1)
    def _():
        write_payload(right_ref, value, bound)


def first_sums(w_part, cot, n_col, dep):
    rows, heads = w_part.shape
    shard = rows // n_col
    keep = cot.shape[1]
    payload = pl.BlockSpec((shard + HEADER, keep), lambda i: (0, 0))
    return pl.pallas_call(
        partial_kernel,
        grid=(n_col,),
        out_shape=[
            shape((rows, keep), F32),
            shape((n_col * 8, 128), F32),
            shape((shard + HEADER, keep), BF16),
            shape((shard + HEADER, keep), BF16),
        ],
        in_specs=[
            pl.BlockSpec((shard, heads), lambda i: (i, 0)),
            pl.BlockSpec((heads, keep), lambda i: (0, 0)),
            ANY,
        ],
        out_specs=[
            pl.BlockSpec((shard, keep), lambda i: (i, 0)),
            pl.BlockSpec((8, 128), lambda i: (i, 0)),
            payload,
            payload,
        ],
        compiler_params=PARAMS,
        cost_estimate=cost(2 * rows * heads * keep, 2 * rows * heads + 4 * rows * keep),
        name="grad_kept_partial",
    )(w_part, cot, dep)


def pass_on_kernel(blocks, at_ref, g_r, b_r, came_r, head_r, g_l, b_l, came_l, head_l, dep_ref, out_r, out_l):
    i = pl.program_id(0)
    sub = came_r.shape[0]
    rows = pl.ds(pl.multiple_of(i * sub, 16), sub)
    for g, b, came, head, out in ((g_r, b_r, came_r, head_r, out_r), (g_l, b_l, came_l, head_l, out_l)):
        undo, bound = read_header(head[...])
        value = g[...] + root(came[...], undo[0:1, 0:1])
        expo = exponent(b[...] + bound)
        out[rows, :] = power(value, jnp.exp2(expo)[0:1, 0:1])

        @pl.when(i == 0)
        def _():
            write_header(out, expo)


def pass_on(numbers, first, sums, bounds, came_r, came_l, dep, blocks):
    shard = came_r.shape[0] - HEADER
    keep = came_r.shape[1]
    sub = shard // blocks
    whole = pl.BlockSpec((shard + HEADER, keep), lambda i, at: (0, 0))
    came = [
        pl.BlockSpec((sub, keep), lambda i, at: (i, 0)),
        pl.BlockSpec((HEADER, keep), lambda i, at: (shard // HEADER, 0)),
    ]

    def own(n):
        return [
            pl.BlockSpec((sub, keep), lambda i, at: (at[n] * blocks + i, 0)),
            pl.BlockSpec((8, 128), lambda i, at: (at[n], 0)),
        ]

    return pl.pallas_call(
        functools.partial(pass_on_kernel, blocks),
        grid_spec=pltpu.PrefetchScalarGridSpec(
            num_scalar_prefetch=1,
            grid=(blocks,),
            in_specs=own(first) + came + own(first + 1) + came + [ANY],
            out_specs=[whole, whole],
        ),
        out_shape=[shape((shard + HEADER, keep), BF16)] * 2,
        compiler_params=PARAMS,
        cost_estimate=cost(0, 16 * shard * keep),
        name="grad_kept_pass_on",
    )(numbers, sums, bounds, came_r, came_r, sums, bounds, came_l, came_l, dep)


def last_kernel(at_ref, g_ref, r_ref, rh_ref, l_ref, lh_ref, base_ref, dep_ref, out_ref):
    undo_r, _ = read_header(rh_ref[...])
    undo_l, _ = read_header(lh_ref[...])
    total = root(r_ref[...], undo_r[0:1, 0:1]) + root(l_ref[...], undo_l[0:1, 0:1])
    out_ref[0] = g_ref[...] + total


def last_sums(numbers, sums, came_r, came_l, base, dep, part, parts, blocks):
    shard = came_r.shape[0] - HEADER
    keep = came_r.shape[1]
    sub = shard // blocks
    rows = pl.BlockSpec((sub, keep), lambda b, at: (b, 0))
    head = pl.BlockSpec((HEADER, keep), lambda b, at: (shard // HEADER, 0))
    return pl.pallas_call(
        last_kernel,
        grid_spec=pltpu.PrefetchScalarGridSpec(
            num_scalar_prefetch=1,
            grid=(blocks,),
            in_specs=[
                pl.BlockSpec((sub, keep), lambda b, at: (at[2] * blocks + b, 0)),
                rows,
                head,
                rows,
                head,
                ANY,
                ANY,
            ],
            out_specs=pl.BlockSpec((1, sub, keep), lambda b, at: (b * parts + part, 0, 0)),
        ),
        out_shape=shape((blocks * parts, sub, keep), F32),
        input_output_aliases={6: 0} if part else {},
        compiler_params=PARAMS,
        cost_estimate=cost(0, 12 * shard * keep),
        name="grad_kept_last",
    )(numbers, sums, came_r, came_r, came_l, came_l, base, dep)


def fetch(refs, source, target, sem):
    for j, ref in enumerate(refs):

        @pl.when(source == j)
        def _():
            pltpu.make_async_copy(ref, target, sem).start()

    return pltpu.make_async_copy(refs[0], target, sem)


def give_kernel(n_col, n_half, where_ref, dep_ref, *refs):
    sources, (out_ref, sem) = refs[: 2 * n_col - 1], refs[2 * n_col - 1 :]
    other = 1 - where_ref[0]
    shard = sources[0].shape[0]
    waits = [
        fetch(
            sources,
            other * n_half + i - where_ref[2] + n_col - 1,
            out_ref.at[pl.ds(i * shard, shard), :],
            sem.at[i],
        )
        for i in range(n_half)
    ]
    for wait in waits:
        wait.wait()


def other_half(where, line, n_col, n_half, dep):
    shard, keep = line[0].shape
    return pl.pallas_call(
        functools.partial(give_kernel, n_col, n_half),
        out_shape=shape((n_half * shard, keep), BF16),
        in_specs=[SMEM, ANY] + [ANY] * len(line),
        out_specs=VMEM,
        scratch_shapes=[pltpu.SemaphoreType.DMA((n_half,))],
        compiler_params=PARAMS,
        cost_estimate=cost(0, 4 * n_half * shard * keep),
        name="half_for_other_core",
    )(where, dep, *line)


def weight_kernel(n_col, n_half, n_row, where_ref, cot_ref, cot_other_ref, other_ref, dep_ref, *refs):
    sources = refs[: 2 * n_col - 1]
    own_ref, send_refs = refs[2 * n_col - 1], refs[2 * n_col : 2 * n_col + n_row - 1]
    mine_ref, total_ref, sem = refs[2 * n_col + n_row - 1 :]
    dp, row, col = where_ref[0], where_ref[1], where_ref[2]
    shard = sources[0].shape[0]
    waits = [
        fetch(
            sources,
            dp * n_half + i - col + n_col - 1,
            mine_ref.at[pl.ds(i * shard, shard), :],
            sem.at[i],
        )
        for i in range(n_half)
    ]
    for wait in waits:
        wait.wait()
    sub = own_ref.shape[0]
    bound = jnp.zeros((8, 128), F32)
    for step in range(n_row):
        rows = pl.ds(pl.multiple_of((row ^ step) * sub, 16), sub)
        value = dot(mine_ref[rows, :], cot_ref[...], 1, 1) + dot(other_ref[rows, :], cot_other_ref[...], 1, 1)
        if step == 0:
            own_ref[...] = value
        else:
            total_ref[step - 1] = value
            bound = jnp.maximum(bound, tile_max(value))
    for step in range(1, n_row):
        write_payload(send_refs[step - 1], total_ref[step - 1], bound)


def weight_partial(where, cot, cot_other, other, line, n_col, n_half, n_row, dep):
    half, keep = other.shape
    heads = cot.shape[0]
    sub = half // n_row
    return pl.pallas_call(
        functools.partial(weight_kernel, n_col, n_half, n_row),
        out_shape=[shape((sub, heads), F32)] + [shape((sub + HEADER, heads), BF16)] * (n_row - 1),
        in_specs=[SMEM, VMEM, VMEM, VMEM, ANY] + [ANY] * len(line),
        out_specs=[VMEM] * n_row,
        scratch_shapes=[
            pltpu.VMEM((half, keep), BF16),
            pltpu.VMEM((n_row - 1, sub, heads), F32),
            pltpu.SemaphoreType.DMA((n_half,)),
        ],
        compiler_params=PARAMS,
        cost_estimate=cost(4 * half * keep * heads, 4 * half * (keep + heads)),
        name="grad_weight_partial",
    )(where, cot, cot_other, other, dep, *line)


def weight_last_kernel(n_came, *refs):
    own_ref, came_refs, out_ref = refs[0], refs[1 : 1 + n_came], refs[-1]
    rows = own_ref.shape[0]
    total = own_ref[...]
    for came in came_refs:
        undo, _ = read_header(came[rows:, :])
        total = total + root(came[:rows, :], undo[0:1, 0:1])
    out_ref[...] = total


def weight_last(own, came, base, dep, part, parts):
    sub, heads = own.shape
    tile = 256
    rows = pl.BlockSpec((sub, tile), lambda i: (0, i))
    whole = pl.BlockSpec((sub + HEADER, tile), lambda i: (0, i))
    return pl.pallas_call(
        functools.partial(weight_last_kernel, len(came)),
        grid=(heads // tile,),
        out_shape=shape((sub * parts, heads), F32),
        in_specs=[rows] + [whole] * len(came) + [ANY, ANY],
        out_specs=pl.BlockSpec((sub, tile), lambda i: (part, i)),
        input_output_aliases={1 + len(came): 0} if part else {},
        compiler_params=PARAMS,
        cost_estimate=cost(0, 14 * sub * heads),
        name="grad_weight_last",
    )(own, *came, base, dep)


def query_kernel(n_col, parts, where_ref, dep_ref, *refs):
    w_refs = refs[:parts]
    count = 2 * n_col - 1
    lines = [refs[parts + p * count : parts + (p + 1) * count] for p in range(parts)]
    out_ref, panel_ref, sem = refs[parts + parts * count :]
    shard = lines[0][0].shape[0]

    @pl.when(pl.program_id(0) == 0)
    def _():
        waits = [
            fetch(
                lines[p],
                i - where_ref[2] + n_col - 1,
                panel_ref.at[p, pl.ds(i * shard, shard), :],
                sem.at[p, i],
            )
            for p in range(parts)
            for i in range(n_col)
        ]
        for wait in waits:
            wait.wait()

    total = dot(w_refs[0][...], panel_ref[0], 0, 0)
    for p in range(1, parts):
        total = total + dot(w_refs[p][...], panel_ref[p], 0, 0)
    out_ref[...] = total.astype(BF16)


def all_queries(where, w_parts, lines, n_col, dep):
    parts = len(w_parts)
    rows, heads = w_parts[0].shape
    shard, keep = lines[0][0].shape
    tile = 256
    return pl.pallas_call(
        functools.partial(query_kernel, n_col, parts),
        grid=(heads // tile,),
        out_shape=shape((heads, keep), BF16),
        in_specs=[SMEM, ANY]
        + [pl.BlockSpec((rows, tile), lambda i: (0, i))] * parts
        + [ANY] * (len(lines[0]) * parts),
        out_specs=pl.BlockSpec((tile, keep), lambda i: (i, 0)),
        scratch_shapes=[
            pltpu.VMEM((parts, rows, keep), BF16),
            pltpu.SemaphoreType.DMA((parts, n_col)),
        ],
        compiler_params=PARAMS,
        cost_estimate=cost(2 * parts * rows * heads * keep, 2 * parts * rows * (heads + keep)),
        name="queries",
    )(where, dep, *w_parts, *[piece for line in lines for piece in line])


def nothing_kernel(*refs):
    pass


def after(values, deps):
    return pl.pallas_call(
        nothing_kernel,
        out_shape=[shape(v.shape, v.dtype) for v in values],
        in_specs=[ANY] * (len(values) + len(deps)),
        out_specs=[ANY] * len(values),
        input_output_aliases={i: i for i in range(len(values))},
        compiler_params=PARAMS,
        cost_estimate=cost(0, 0),
        name="after",
    )(*values, *deps)


def per_device(tokens, kept_index, w_query, cotangent):
    n_dp, n_row, n_col = (lax.axis_size(a) for a in ("dp", "row", "col"))
    dp, row, col = (lax.axis_index(a) for a in ("dp", "row", "col"))
    seq_x = tokens[0]
    cot = cotangent[0]
    d_dev = seq_x.shape[0]
    w_rows = w_query.shape[0]
    keep_dev = cot.shape[1]
    drift = keep_dev // 4
    parts = 2 if w_rows % 32 == 0 else 1
    sub = w_rows // parts
    blocks = d_dev // w_rows
    n_half = n_col // n_dp

    numbers = [dp, row, col]
    for t in range(2, n_col):
        numbers += [jnp.clip(b, 0, n_col - 1) for b in (n_col - t + col, t - n_col + col)]
    numbers = jnp.stack(numbers).astype(jnp.int32)

    kept, leaving = kept_tokens(seq_x, kept_index, keep_dev, drift, blocks, parts, sub, n_row)
    w_parts = [
        lax.all_gather(w, ("dp", "row"), axis=0, tiled=True) for w in split_rows(w_query, parts, leaving)
    ]
    swap = [(i, i ^ 1) for i in range(n_dp)]
    cot_other = lax.ppermute(cot, "dp", swap)

    def along(value, sources, step):
        return lax.ppermute(value, "col", [(c, c + step) for c in sources])

    from_left = [[k] for k in kept]
    from_right = [[k] for k in kept]
    sums, bounds, right, left = ([None] * parts for _ in range(4))
    sent = []

    def gather_step(p, t):
        if t > 2:
            held = after([from_left[p][-1], from_right[p][-1]], sent[-1:])
            from_left[p][-1], from_right[p][-1] = held
        from_left[p].append(along(from_left[p][-1], range(t - 1, n_col - 1), 1))
        from_right[p].append(along(from_right[p][-1], range(1, n_col - t + 1), -1))

    def reduce_step(p, t, dep):
        if t == 1:
            sums[p], bounds[p], right[p], left[p] = first_sums(w_parts[p], cot, n_col, dep)
        else:
            at = 3 + 2 * (t - 2)
            right[p], left[p] = pass_on(numbers, at, sums[p], bounds[p], right[p], left[p], dep, blocks)
        sent.append(right[p])
        right[p] = along(right[p], range(t), 1)
        left[p] = along(left[p], range(n_col - 1, n_col - 1 - t, -1), -1)

    def weight_step(p, dep):
        line = from_left[p][:0:-1] + [kept[p]] + from_right[p][1:]
        give = other_half(numbers, line, n_col, n_half, dep)
        other = lax.ppermute(give, "dp", swap)
        own, *sends = weight_partial(numbers, cot, cot_other, other, line, n_col, n_half, n_row, sent[-1])
        came = [
            lax.ppermute(send, "row", [(r, r ^ step) for r in range(n_row)])
            for step, send in enumerate(sends, 1)
        ]
        return line, own, came

    for t in (1, 2):
        for p in range(parts):
            gather_step(p, t)
    reduce_step(0, 1, from_left[-1][1])
    for t in range(3, n_col):
        for p in range(parts):
            gather_step(p, t)
            if t - 1 + p < n_col:
                reduce_step(0, t - 1 + p, from_left[p][t - 1])
    for t in range(len(sent) + 1, n_col):
        reduce_step(0, t, sent[-1])
    lines, owns, cames = [], [], []
    for p in range(parts):
        if p > 0:
            reduce_step(p, 1, sent[-1])
        line, own, came = weight_step(p, sent[-1])
        lines.append(line)
        owns.append(own)
        cames.append(came)
        if p > 0:
            for t in range(2, n_col):
                reduce_step(p, t, own if t > 2 else sent[-1])
    queries = all_queries(numbers, w_parts, lines, n_col, sent[-1])
    grad_kept, grad_weight = kept[0], kept[0]
    for p in range(parts):
        dep = queries if p == parts - 1 else sent[-1]
        grad_kept = last_sums(numbers, sums[p], right[p], left[p], grad_kept, dep, p, parts, blocks)
        grad_weight = weight_last(owns[p], cames[p], grad_weight, dep, p, parts)
    return (queries[None], grad_kept.reshape(1, d_dev, keep_dev), grad_weight)


def solution(mesh):
    in_specs = (
        P("dp", "col", "row"),
        P("dp", None),
        P(("dp", "row"), "col"),
        P("dp", "col", "row"),
    )
    out_specs = (P("dp", "col", "row"), P("dp", "col", "row"), P(("dp", "row"), "col"))
    return jax.shard_map(
        per_device, mesh=mesh, in_specs=in_specs, out_specs=out_specs, check_vma=False
    )
```

```python
import functools

import jax
import jax.numpy as jnp
from jax import lax
from jax.experimental import pallas as pl
from jax.experimental.pallas import tpu as pltpu
from jax.sharding import PartitionSpec as P

HEADER = 16
OFFSET = 128.0
F32 = jnp.float32
BF16 = jnp.bfloat16
ANY = pl.BlockSpec(memory_space=pl.ANY)
VMEM = pl.BlockSpec(memory_space=pltpu.VMEM)
SMEM = pl.BlockSpec(memory_space=pltpu.SMEM)


def call(kernel, name, out_shape, in_specs, args, out_specs=None, scratch=(), aliases=None, flops=0, mib=14):
    moved = sum(a.size * a.dtype.itemsize for a, s in zip(args, in_specs) if s is VMEM)
    return pl.pallas_call(
        kernel,
        out_shape=out_shape,
        in_specs=in_specs,
        out_specs=out_specs if out_specs is not None else [VMEM] * len(out_shape),
        scratch_shapes=scratch,
        input_output_aliases=aliases or {},
        compiler_params=pltpu.CompilerParams(vmem_limit_bytes=mib * 2**20),
        cost_estimate=pl.CostEstimate(flops=int(flops), bytes_accessed=int(moved), transcendentals=0),
        name=name,
    )(*args)


def shape(dims, dtype):
    return jax.ShapeDtypeStruct(dims, dtype)


def dot(a, b, ca, cb):
    return lax.dot_general(a, b, (((ca,), (cb,)), ((), ())), preferred_element_type=F32)


def span(start, size):
    return pl.ds(pl.multiple_of(start, 16), size)


def chunks(rows):
    size = 32 if rows % 32 == 0 else 16
    return size, rows // size


def exponent(bound):
    return jnp.clip(jnp.floor(14.99 - jnp.log2(jnp.maximum(bound, 1e-30))), -100.0, 100.0)


def power(values, scale):
    v = values * scale
    square = v * v
    fourth = square * square
    return (fourth * square * (v * jnp.abs(v))).astype(BF16)


def root(code, scale):
    y = code.astype(F32)
    quarter = lax.rsqrt(lax.rsqrt(jnp.maximum(jnp.abs(y), 1e-37)))
    size = quarter * lax.rsqrt(quarter) * scale
    return jnp.where(y > 0.0, size, jnp.where(y < 0.0, -size, 0.0))


def tile_max(values):
    most = jnp.max(jnp.abs(values), axis=0, keepdims=True)
    return jnp.broadcast_to(jnp.max(most, axis=1, keepdims=True), (8, 128))


def write_header(out_ref, expo):
    rows = out_ref.shape[0] - HEADER
    code = jnp.broadcast_to((expo + OFFSET)[0:1, 0:1], (HEADER, out_ref.shape[1]))
    out_ref[rows:, :] = code.astype(BF16)


def write_payload(out_ref, value_of, bound):
    expo = exponent(bound)
    scale = jnp.exp2(expo)[0:1, 0:1]
    size, count = chunks(out_ref.shape[0] - HEADER)

    @pl.loop(0, count)
    def _(i):
        out_ref[span(i * size, size), :] = power(value_of(i * size, size), scale)

    write_header(out_ref, expo)


def read_header(came_ref):
    rows = came_ref.shape[0] - HEADER
    code = came_ref[rows:, :][0:8, 0:128].astype(F32)
    came = code > 0.0
    expo = jnp.where(came, code - OFFSET, 0.0)
    return jnp.exp2(-expo)[0:1, 0:1], jnp.where(came, jnp.exp2(15.0 - expo), 0.0)


def pick_kernel(blocks, n_row, index_ref, x_ref, leaving_ref, *refs):
    parts = len(refs) - 3
    out_refs, (rows_ref, onehot_ref, sem) = refs[:parts], refs[parts:]
    d_dev, seq_dev = rows_ref.shape
    drift, keep_dev = leaving_ref.shape[1], out_refs[0].shape[1]
    sub = d_dev // (blocks * parts)

    def copy(i):
        rows = pl.ds(i * sub, sub)
        return pltpu.make_async_copy(x_ref.at[rows, :], rows_ref.at[rows, :], sem.at[i])

    for i in range(blocks * parts):
        copy(i).start()
    row = lax.axis_index("row")

    def onehot(first, count):
        index = index_ref[:, pl.ds(pl.multiple_of(first, 128), count)] - row * seq_dev
        positions = lax.broadcasted_iota(jnp.int32, (seq_dev, count), 0)
        return (positions == index).astype(F32).astype(BF16)

    onehot_ref[:, :keep_dev] = onehot(row * keep_dev, keep_dev)
    onehot_ref[:, keep_dev:] = onehot(jnp.minimum(row + 1, n_row - 1) * keep_dev, drift)
    for i in range(blocks * parts):
        copy(i).wait()
        picked = dot(rows_ref[pl.ds(i * sub, sub), :], onehot_ref[...], 1, 0).astype(BF16)
        out_refs[i % parts][pl.ds((i // parts) * sub, sub), :] = picked[:, :keep_dev]
        leaving_ref[pl.ds(i * sub, sub), :] = picked[:, keep_dev:]


def add_arrived_kernel(blocks, arrived_ref, *refs):
    parts = len(refs) // 2
    in_refs, out_refs = refs[:parts], refs[parts:]
    drift = arrived_ref.shape[1]
    sub = in_refs[0].shape[0] // blocks
    for b in range(blocks):
        for p in range(parts):
            rows = pl.ds(b * sub, sub)
            came = arrived_ref[pl.ds((b * parts + p) * sub, sub), :]
            out_refs[p][rows, :drift] = in_refs[p][rows, :drift] + came


def split_kernel(w_ref, dep_ref, *refs):
    out_refs, sem = refs[:-1], refs[-1]
    sub = out_refs[0].shape[0]
    copies = [
        pltpu.make_async_copy(w_ref.at[pl.ds(p * sub, sub), :], out_ref, sem.at[p])
        for p, out_ref in enumerate(out_refs)
    ]
    for copy in copies:
        copy.start()
    for copy in copies:
        copy.wait()


def nothing_kernel(*refs):
    pass


def after(values, deps):
    return call(
        nothing_kernel,
        "after",
        [shape(v.shape, v.dtype) for v in values],
        [ANY] * (len(values) + len(deps)),
        (*values, *deps),
        out_specs=[ANY] * len(values),
        aliases={i: i for i in range(len(values))},
        mib=1,
    )


def first_kernel(n_dp, n_row, n_col, *refs):
    pieces, (cot_ref, w_ref, sums_ref, bounds_ref, right_ref, left_ref) = refs[: n_dp * n_row], refs[-6:]
    dp, row = lax.axis_index("dp"), lax.axis_index("row")
    sub = pieces[0].shape[0]
    for n, piece in enumerate(pieces):
        block = (dp if n < n_row else 1 - dp) * n_row + (row ^ (n % n_row))
        w_ref[span(block * sub, sub), :] = piece[...]
    shard = w_ref.shape[0] // n_col
    for i in range(n_col):
        rows = pl.ds(i * shard, shard)
        value = dot(w_ref[rows, :], cot_ref[...], 1, 0)
        sums_ref[rows, :] = value
        bounds_ref[pl.ds(i * 8, 8), :] = tile_max(value)
    for out_ref, i in ((right_ref, n_col - 1), (left_ref, 0)):
        write_payload(
            out_ref,
            lambda first, size, i=i: sums_ref[span(i * shard + first, size), :],
            bounds_ref[pl.ds(i * 8, 8), :],
        )


def first_sums(pieces, cot, n_dp, n_row, n_col, deps):
    sub, heads = pieces[0].shape
    keep = cot.shape[1]
    rows = sub * n_dp * n_row
    payload = shape((rows // n_col + HEADER, keep), BF16)

    def kernel(*refs):
        first_kernel(n_dp, n_row, n_col, *refs[: n_dp * n_row], refs[n_dp * n_row], *refs[-5:])

    return call(
        kernel,
        "grad_kept_first",
        [shape((rows, heads), BF16), shape((rows, keep), F32), shape((n_col * 8, 128), F32), payload, payload],
        [VMEM] * (len(pieces) + 1) + [ANY] * len(deps),
        (*pieces, cot, *deps),
        flops=2 * rows * heads * keep,
    )


def pass_on_kernel(n_col, t, sums_ref, bounds_ref, came_r, came_l, dep_ref, out_r, out_l):
    shard = came_r.shape[0] - HEADER
    col = lax.axis_index("col")
    for block, came, out in ((n_col - t + col, came_r, out_r), (t - n_col + col, came_l, out_l)):
        block = jnp.clip(block, 0, n_col - 1)
        undo, bound = read_header(came)
        write_payload(
            out,
            lambda first, size, block=block, came=came, undo=undo: (
                sums_ref[span(block * shard + first, size), :] + root(came[span(first, size), :], undo)
            ),
            bounds_ref[pl.ds(pl.multiple_of(block * 8, 8), 8), :] + bound,
        )


def pass_on(n_col, t, sums, bounds, came_r, came_l, dep):
    payload = shape(came_r.shape, BF16)
    return call(
        functools.partial(pass_on_kernel, n_col, t),
        "grad_kept_pass_on",
        [payload, payload],
        [VMEM] * 4 + [ANY],
        (sums, bounds, came_r, came_l, dep),
        flops=20 * came_r.size,
    )


def last_kernel(part, parts, blocks, sums_ref, r_ref, l_ref, base_ref, dep_ref, out_ref, total_ref, sem):
    shard = r_ref.shape[0] - HEADER
    sub = shard // blocks
    first = lax.axis_index("col") * shard
    undo_r, _ = read_header(r_ref)
    undo_l, _ = read_header(l_ref)
    size, count = chunks(sub)
    copies = []
    for b in range(blocks):

        @pl.loop(0, count)
        def _(i):
            at = b * sub + i * size
            rows = span(at, size)
            came = root(r_ref[rows, :], undo_r) + root(l_ref[rows, :], undo_l)
            total_ref[rows, :] = sums_ref[span(first + at, size), :] + came

        copies.append(
            pltpu.make_async_copy(
                total_ref.at[pl.ds(b * sub, sub), :], out_ref.at[b * parts + part], sem.at[b]
            )
        )
        copies[-1].start()
    for copy in copies:
        copy.wait()


def last_sums(sums, came_r, came_l, base, dep, part, parts, blocks):
    shard, keep = came_r.shape[0] - HEADER, came_r.shape[1]
    return call(
        functools.partial(last_kernel, part, parts, blocks),
        "grad_kept_last",
        shape((blocks * parts, shard // blocks, keep), F32),
        [VMEM] * 3 + [ANY] * 2,
        (sums, came_r, came_l, base, dep),
        out_specs=ANY,
        scratch=[pltpu.VMEM((shard, keep), F32), pltpu.SemaphoreType.DMA((blocks,))],
        aliases={3: 0} if part else None,
        flops=20 * shard * keep,
    )


def each_shard(line):
    n_col = (len(line) + 1) // 2
    col = lax.axis_index("col")
    for n, ref in enumerate(line):
        shard = col + n - (n_col - 1)
        yield (shard >= 0) & (shard < n_col), shard, ref


def half_kernel(n_half, *refs):
    line, out_ref = refs[:-2], refs[-1]
    other = 1 - lax.axis_index("dp")
    for came, shard, ref in each_shard(line):
        rows = ref.shape[0]

        @pl.when(came & (shard >= other * n_half) & (shard < (other + 1) * n_half))
        def _():
            out_ref[span((shard - other * n_half) * rows, rows), :] = ref[...]


def other_half(line, n_half, dep):
    rows, keep = line[0].shape
    return call(
        functools.partial(half_kernel, n_half),
        "half_for_other_core",
        shape((n_half * rows, keep), BF16),
        [VMEM] * len(line) + [ANY],
        (*line, dep),
        out_specs=VMEM,
    )


def weight_kernel(n_half, n_row, cot_ref, cot_other_ref, other_ref, *refs):
    count = len(refs) - n_row - 3
    line, own_ref, send_refs = refs[:count], refs[count + 1], refs[count + 2 : count + 1 + n_row]
    mine_ref, total_ref = refs[-2:]
    dp, row = lax.axis_index("dp"), lax.axis_index("row")
    for came, shard, ref in each_shard(line):
        rows = ref.shape[0]

        @pl.when(came & (shard >= dp * n_half) & (shard < (dp + 1) * n_half))
        def _():
            mine_ref[span((shard - dp * n_half) * rows, rows), :] = ref[...]

    sub = own_ref.shape[0]
    bound = jnp.zeros((8, 128), F32)
    for step in range(n_row):
        rows = span((row ^ step) * sub, sub)
        value = dot(mine_ref[rows, :], cot_ref[...], 1, 1) + dot(other_ref[rows, :], cot_other_ref[...], 1, 1)
        if step == 0:
            own_ref[...] = value
        else:
            total_ref[step - 1] = value
            bound = jnp.maximum(bound, tile_max(value))
    for step in range(1, n_row):
        write_payload(
            send_refs[step - 1],
            lambda first, size, step=step: total_ref[step - 1, span(first, size), :],
            bound,
        )


def weight_partial(cot, cot_other, other, line, n_half, n_row, dep):
    half, keep = other.shape
    heads = cot.shape[0]
    sub = half // n_row
    return call(
        functools.partial(weight_kernel, n_half, n_row),
        "grad_weight_partial",
        [shape((sub, heads), F32)] + [shape((sub + HEADER, heads), BF16)] * (n_row - 1),
        [VMEM] * (3 + len(line)) + [ANY],
        (cot, cot_other, other, *line, dep),
        scratch=[pltpu.VMEM((half, keep), BF16), pltpu.VMEM((n_row - 1, sub, heads), F32)],
        flops=4 * half * keep * heads,
        mib=20,
    )


def weight_last_kernel(n_came, part, own_ref, *refs):
    came_refs, (out_ref, total_ref, sem) = refs[:n_came], refs[-3:]
    sub = own_ref.shape[0]
    undo = [read_header(came)[0] for came in came_refs]
    size = 16
    steps = sub // size
    copies = []
    for first, last in ((0, steps // 2), (steps // 2, steps)):

        @pl.loop(first, last)
        def _(i):
            rows = span(i * size, size)
            total = own_ref[rows, :]
            for came, scale in zip(came_refs, undo):
                total = total + root(came[rows, :], scale)
            total_ref[rows, :] = total

        rows = pl.ds(first * size, (last - first) * size)
        target = out_ref.at[pl.ds(part * sub + first * size, (last - first) * size), :]
        copies.append(pltpu.make_async_copy(total_ref.at[rows, :], target, sem.at[len(copies)]))
        copies[-1].start()
    for copy in copies:
        copy.wait()


def weight_last(own, came, base, dep, part, parts):
    sub, heads = own.shape
    return call(
        functools.partial(weight_last_kernel, len(came), part),
        "grad_weight_last",
        shape((sub * parts, heads), F32),
        [VMEM] * (1 + len(came)) + [ANY] * 2,
        (own, *came, base, dep),
        out_specs=ANY,
        scratch=[pltpu.VMEM((sub, heads), F32), pltpu.SemaphoreType.DMA((2,))],
        aliases={1 + len(came): 0} if part else None,
        flops=20 * sub * heads * len(came),
    )


def query_kernel(parts, *refs):
    w_refs = refs[:parts]
    count = (len(refs) - parts - 3) // parts
    lines = [refs[parts + p * count : parts + (p + 1) * count] for p in range(parts)]
    out_ref, panel_ref = refs[-2:]
    for p, line in enumerate(lines):
        for came, shard, ref in each_shard(line):
            rows = ref.shape[0]

            @pl.when(came)
            def _():
                panel_ref[p, span(shard * rows, rows), :] = ref[...]

    tile = 256
    for i in range(out_ref.shape[0] // tile):
        heads = pl.ds(i * tile, tile)
        total = dot(w_refs[0][:, heads], panel_ref[0], 0, 0)
        for p in range(1, parts):
            total = total + dot(w_refs[p][:, heads], panel_ref[p], 0, 0)
        out_ref[heads, :] = total.astype(BF16)


def all_queries(w_parts, lines, dep):
    parts = len(w_parts)
    rows, heads = w_parts[0].shape
    keep = lines[0][0].shape[1]
    return call(
        functools.partial(query_kernel, parts),
        "queries",
        shape((heads, keep), BF16),
        [VMEM] * (parts + len(lines[0]) * parts) + [ANY],
        (*w_parts, *[piece for line in lines for piece in line], dep),
        out_specs=VMEM,
        scratch=[pltpu.VMEM((parts, rows, keep), BF16)],
        flops=2 * parts * rows * heads * keep,
        mib=20,
    )


def per_device(tokens, kept_index, w_query, cotangent):
    n_dp, n_row, n_col = (lax.axis_size(a) for a in ("dp", "row", "col"))
    seq_x = tokens[0]
    cot = cotangent[0]
    d_dev, seq_dev = seq_x.shape
    w_rows, heads = w_query.shape
    keep_dev = cot.shape[1]
    drift = keep_dev // 4
    parts = 2 if w_rows % 32 == 0 else 1
    sub = w_rows // parts
    blocks = d_dev // w_rows
    shard = blocks * sub
    n_half = n_col // n_dp

    def to_row(value, step):
        return lax.ppermute(value, "row", [(r, r ^ step) for r in range(n_row)])

    def to_core(value):
        return lax.ppermute(value, "dp", [(i, i ^ 1) for i in range(n_dp)])

    def along(value, sources, step):
        return lax.ppermute(value, "col", [(c, c + step) for c in sources])

    leaving, *picked = call(
        functools.partial(pick_kernel, blocks, n_row),
        "pick",
        [shape((d_dev, drift), BF16)] + [shape((shard, keep_dev), BF16)] * parts,
        [VMEM, ANY],
        (kept_index, seq_x),
        scratch=[
            pltpu.VMEM((d_dev, seq_dev), BF16),
            pltpu.VMEM((seq_dev, keep_dev + drift), BF16),
            pltpu.SemaphoreType.DMA((blocks * parts,)),
        ],
        flops=2 * d_dev * seq_dev * (keep_dev + drift),
    )
    arrived = lax.ppermute(leaving, "row", [(r, r + 1) for r in range(n_row - 1)])
    own_w = list(call(
        split_kernel,
        "split_rows",
        [shape((sub, heads), BF16)] * parts,
        [ANY, ANY],
        (w_query, leaving),
        scratch=[pltpu.SemaphoreType.DMA((parts,))],
    ))
    cot_other = to_core(cot)
    pieces = []
    for p in range(parts):
        if p > 0:
            (own_w[p],) = after([own_w[p]], pieces[0][1:n_row])
        mine = [own_w[p]] + [to_row(own_w[p], step) for step in range(1, n_row)]
        pieces.append(mine + [to_core(m) for m in mine])
    kept = call(
        functools.partial(add_arrived_kernel, blocks),
        "add_arrived",
        [shape((shard, keep_dev), BF16)] * parts,
        [VMEM] * (1 + parts),
        (arrived, *picked),
        aliases={1 + p: p for p in range(parts)},
    )

    from_left = [[k] for k in kept]
    from_right = [[k] for k in kept]
    w_parts, sums, bounds, right, left, owns, cames = ([None] * parts for _ in range(7))
    token = None

    def line_of(p):
        return from_left[p][:0:-1] + [kept[p]] + from_right[p][1:]

    def gather(p, t):
        nonlocal token
        if t > 2:
            held = after([from_left[p][-1], from_right[p][-1]], [token])
            from_left[p][-1], from_right[p][-1] = held
            token = held[0]
        from_left[p].append(along(from_left[p][-1], range(t - 1, n_col - 1), 1))
        from_right[p].append(along(from_right[p][-1], range(1, n_col - t + 1), -1))

    def pass_sums(p, t):
        nonlocal token
        if t == 1:
            deps = [token] if token is not None else [f[q][1] for q in range(parts) for f in (from_left, from_right)]
            w_parts[p], sums[p], bounds[p], right[p], left[p] = first_sums(
                pieces[p], cot, n_dp, n_row, n_col, deps
            )
        else:
            right[p], left[p] = pass_on(n_col, t, sums[p], bounds[p], right[p], left[p], token)
        token = right[p]
        right[p] = along(right[p], range(t), 1)
        left[p] = along(left[p], range(n_col - 1, n_col - 1 - t, -1), -1)

    def weigh(p):
        nonlocal token
        give = other_half(line_of(p), n_half, token)
        owns[p], *sends = weight_partial(cot, cot_other, to_core(give), line_of(p), n_half, n_row, give)
        token = owns[p]
        cames[p] = [to_row(send, step) for step, send in enumerate(sends, 1)]

    last = parts - 1
    for t in (1, 2):
        for p in range(parts):
            gather(p, t)
    pass_sums(0, 1)
    for t in range(3, n_col):
        gather(0, t)
        pass_sums(0, t - 1)
        if parts > 1:
            gather(1, t)
            pass_sums(1, t - 2)
    pass_sums(0, n_col - 1)
    weigh(0)
    if parts > 1:
        pass_sums(1, n_col - 2)
        weigh(1)
        pass_sums(1, n_col - 1)
    queries = all_queries(w_parts, [line_of(p) for p in range(parts)], token)
    grad_kept, grad_weight = leaving, leaving
    for p in range(parts):
        grad_kept = last_sums(sums[p], right[p], left[p], grad_kept, queries, p, parts, blocks)
        grad_weight = weight_last(owns[p], cames[p], grad_weight, queries, p, parts)
    return (queries[None], grad_kept.reshape(1, d_dev, keep_dev), grad_weight)


def solution(mesh):
    in_specs = (
        P("dp", "col", "row"),
        P("dp", None),
        P(("dp", "row"), "col"),
        P("dp", "col", "row"),
    )
    out_specs = (P("dp", "col", "row"), P("dp", "col", "row"), P(("dp", "row"), "col"))
    return jax.shard_map(
        per_device, mesh=mesh, in_specs=in_specs, out_specs=out_specs, check_vma=False
    )
```

```python
import functools

import jax
import jax.numpy as jnp
from jax import lax
from jax.experimental import pallas as pl
from jax.experimental.pallas import tpu as pltpu
from jax.sharding import PartitionSpec as P

HEADER = 16
OFFSET = 128.0
F32 = jnp.float32
BF16 = jnp.bfloat16
ANY = pl.BlockSpec(memory_space=pl.ANY)
VMEM = pl.BlockSpec(memory_space=pltpu.VMEM)
SMEM = pl.BlockSpec(memory_space=pltpu.SMEM)


def call(kernel, name, out_shape, in_specs, args, out_specs=None, scratch=(), aliases=None, flops=0, mib=14):
    moved = sum(a.size * a.dtype.itemsize for a, s in zip(args, in_specs) if s is VMEM)
    return pl.pallas_call(
        kernel,
        out_shape=out_shape,
        in_specs=in_specs,
        out_specs=out_specs if out_specs is not None else [VMEM] * len(out_shape),
        scratch_shapes=scratch,
        input_output_aliases=aliases or {},
        compiler_params=pltpu.CompilerParams(vmem_limit_bytes=mib * 2**20),
        cost_estimate=pl.CostEstimate(flops=1, bytes_accessed=1, transcendentals=0),
        name=name,
    )(*args)


def shape(dims, dtype):
    return jax.ShapeDtypeStruct(dims, dtype)


def dot(a, b, ca, cb):
    return lax.dot_general(a, b, (((ca,), (cb,)), ((), ())), preferred_element_type=F32)


def span(start, size):
    return pl.ds(pl.multiple_of(start, 16), size)


def chunks(rows):
    size = 32 if rows % 32 == 0 else 16
    return size, rows // size


def exponent(bound):
    return jnp.clip(jnp.floor(14.99 - jnp.log2(jnp.maximum(bound, 1e-30))), -100.0, 100.0)


def power(values, scale):
    v = values * scale
    square = v * v
    fourth = square * square
    return (fourth * square * (v * jnp.abs(v))).astype(BF16)


def root(code, scale):
    y = code.astype(F32)
    quarter = lax.rsqrt(lax.rsqrt(jnp.maximum(jnp.abs(y), 1e-37)))
    size = quarter * lax.rsqrt(quarter) * scale
    return jnp.where(y > 0.0, size, jnp.where(y < 0.0, -size, 0.0))


def tile_max(values):
    most = jnp.max(jnp.abs(values), axis=0, keepdims=True)
    return jnp.broadcast_to(jnp.max(most, axis=1, keepdims=True), (8, 128))


def write_header(out_ref, expo):
    rows = out_ref.shape[0] - HEADER
    code = jnp.broadcast_to((expo + OFFSET)[0:1, 0:1], (HEADER, out_ref.shape[1]))
    out_ref[rows:, :] = code.astype(BF16)


def write_payload(out_ref, value_of, bound):
    expo = exponent(bound)
    scale = jnp.exp2(expo)[0:1, 0:1]
    size, count = chunks(out_ref.shape[0] - HEADER)

    @pl.loop(0, count)
    def _(i):
        out_ref[span(i * size, size), :] = power(value_of(i * size, size), scale)

    write_header(out_ref, expo)


def read_header(came_ref):
    rows = came_ref.shape[0] - HEADER
    code = came_ref[rows:, :][0:8, 0:128].astype(F32)
    came = code > 0.0
    expo = jnp.where(came, code - OFFSET, 0.0)
    return jnp.exp2(-expo)[0:1, 0:1], jnp.where(came, jnp.exp2(15.0 - expo), 0.0)


def part_rows(sizes, blocks):
    start = 0
    for size in sizes:
        yield start, size, start * blocks, size * blocks
        start += size


def onehot_of(index_ref, first, count, seq_dev):
    index = index_ref[:, pl.ds(pl.multiple_of(first, 128), count)] - lax.axis_index("row") * seq_dev
    positions = lax.broadcasted_iota(jnp.int32, (seq_dev, count), 0)
    return (positions == index).astype(F32).astype(BF16)


def pick_leaving_kernel(blocks, sizes, n_row, keep_dev, index_ref, x_ref, leaving_ref, rows_ref, onehot_ref, sem):
    d_dev, seq_dev = rows_ref.shape
    step = d_dev // blocks

    def copy(b):
        rows = pl.ds(b * step, step)
        return pltpu.make_async_copy(x_ref.at[rows, :], rows_ref.at[rows, :], sem.at[b])

    for b in range(blocks):
        copy(b).start()
    after = jnp.minimum(lax.axis_index("row") + 1, n_row - 1) * keep_dev
    onehot_ref[...] = onehot_of(index_ref, after, leaving_ref.shape[1], seq_dev)
    for b in range(blocks):
        copy(b).wait()
        for start, size, offset, _ in part_rows(sizes, blocks):
            picked = dot(rows_ref[pl.ds(b * step + start, size), :], onehot_ref[...], 1, 0)
            leaving_ref[pl.ds(offset + b * size, size), :] = picked.astype(BF16)


def pick_own_kernel(blocks, sizes, index_ref, rows_ref, kept_ref, onehot_ref):
    d_dev, seq_dev = rows_ref.shape
    keep_dev = kept_ref.shape[1]
    onehot_ref[...] = onehot_of(index_ref, lax.axis_index("row") * keep_dev, keep_dev, seq_dev)
    for b in range(blocks):
        for start, size, offset, _ in part_rows(sizes, blocks):
            picked = dot(rows_ref[pl.ds(b * (d_dev // blocks) + start, size), :], onehot_ref[...], 1, 0)
            kept_ref[pl.ds(offset + b * size, size), :] = picked.astype(BF16)


def add_arrived_kernel(arrived_ref, in_ref, out_ref):
    drift = arrived_ref.shape[1]
    out_ref[:, :drift] = in_ref[:, :drift] + arrived_ref[...]


def split_kernel(sizes, w_ref, dep_ref, *refs):
    out_refs, sem = refs[:-1], refs[-1]
    copies = [
        pltpu.make_async_copy(w_ref.at[pl.ds(start, size), :], out_refs[p], sem.at[p])
        for p, (start, size, _, _) in enumerate(part_rows(sizes, 1))
    ]
    for copy in copies:
        copy.start()
    for copy in copies:
        copy.wait()


def nothing_kernel(*refs):
    pass


def after(values, deps):
    return call(
        nothing_kernel,
        "after",
        [shape(v.shape, v.dtype) for v in values],
        [ANY] * (len(values) + len(deps)),
        (*values, *deps),
        out_specs=[ANY] * len(values),
        aliases={i: i for i in range(len(values))},
        mib=1,
    )


def collect_kernel(n_row, *refs):
    pieces, out_ref = refs[:n_row], refs[-1]
    row = lax.axis_index("row")
    size = pieces[0].shape[0]
    for step, piece in enumerate(pieces):
        out_ref[span((row ^ step) * size, size), :] = piece[...]


def collect(pieces):
    size, heads = pieces[0].shape
    n_row = len(pieces)
    return call(
        functools.partial(collect_kernel, n_row),
        "collect_rows",
        shape((n_row * size, heads), BF16),
        [VMEM] * n_row,
        pieces,
        out_specs=VMEM,
    )


def partial_into(out_ref, block, n_half, mine_ref, other_ref, cot_ref):
    shard = out_ref.shape[0]
    rows = span((block % n_half) * shard, shard)
    here = block // n_half == lax.axis_index("dp")

    @pl.when(here)
    def _():
        out_ref[...] = dot(mine_ref[rows, :], cot_ref[...], 1, 0)

    @pl.when(jnp.logical_not(here))
    def _():
        out_ref[...] = dot(other_ref[rows, :], cot_ref[...], 1, 0)


def step_kernel(n_col, n_half, t, offset, mine_ref, other_ref, cot_ref, came_r, came_l, dep_ref, out_r, out_l, term_ref):
    shard = out_r.shape[0] - HEADER
    col = lax.axis_index("col")
    ways = ((col, n_col - t + col, came_r, out_r), (n_col - 1 - col, t - n_col + col, came_l, out_l))
    for place, block, came, out in ways:

        @pl.when(place >= t)
        def _():
            out[:shard, :] = came[pl.ds(offset, shard), :]

        @pl.when(place < t)
        def _():
            partial_into(term_ref, block, n_half, mine_ref, other_ref, cot_ref)
            bound = tile_max(term_ref[...])
            if t == 1:
                write_payload(out, lambda first, size: term_ref[span(first, size), :], bound)
            else:
                undo, came_bound = read_header(came)

                def total(first, size):
                    rows = span(first, size)
                    return term_ref[rows, :] + root(came[rows, :], undo)

                write_payload(out, total, bound + came_bound)


def line_step(n_col, n_half, t, offset, shard, mine, other, cot, came_r, came_l, dep):
    keep = cot.shape[1]
    payload = shape((shard + HEADER, keep), BF16)
    return call(
        functools.partial(step_kernel, n_col, n_half, t, offset),
        "line_step",
        [payload, payload],
        [VMEM] * 5 + [ANY],
        (mine, other, cot, came_r, came_l, dep),
        scratch=[pltpu.VMEM((shard, keep), F32)],
    )


def last_kernel(start, size, blocks, n_half, mine_ref, other_ref, cot_ref, r_ref, l_ref, base_ref, dep_ref, out_ref, total_ref, sem):
    step = out_ref.shape[0] // blocks
    partial_into(total_ref, lax.axis_index("col"), n_half, mine_ref, other_ref, cot_ref)
    undo_r, _ = read_header(r_ref)
    undo_l, _ = read_header(l_ref)
    few, count = chunks(size)
    copies = []
    for b in range(blocks):

        @pl.loop(0, count)
        def _(i):
            rows = span(b * size + i * few, few)
            came = root(r_ref[rows, :], undo_r) + root(l_ref[rows, :], undo_l)
            total_ref[rows, :] = total_ref[rows, :] + came

        target = out_ref.at[pl.ds(b * step + start, size), :]
        copies.append(pltpu.make_async_copy(total_ref.at[pl.ds(b * size, size), :], target, sem.at[b]))
        copies[-1].start()
    for copy in copies:
        copy.wait()


def last_sums(mine, other, cot, came_r, came_l, base, dep, start, size, blocks, n_half, d_dev):
    shard, keep = came_r.shape[0] - HEADER, came_r.shape[1]
    return call(
        functools.partial(last_kernel, start, size, blocks, n_half),
        "grad_kept_last",
        shape((d_dev, keep), F32),
        [VMEM] * 5 + [ANY] * 2,
        (mine, other, cot, came_r, came_l, base, dep),
        out_specs=ANY,
        scratch=[pltpu.VMEM((shard, keep), F32), pltpu.SemaphoreType.DMA((blocks,))],
        aliases={5: 0} if start else None,
    )


def each_shard(line, offset, rows):
    n_col = (len(line) + 1) // 2
    col = lax.axis_index("col")
    for n, ref in enumerate(line):
        shard = col + n - (n_col - 1)
        whole = abs(n - (n_col - 1)) < 2
        yield (shard >= 0) & (shard < n_col), shard, ref.at[pl.ds(offset if whole else 0, rows), :]


def half_kernel(n_half, offset, rows, *refs):
    line, out_ref = refs[:-2], refs[-1]
    other = 1 - lax.axis_index("dp")
    for came, shard, ref in each_shard(line, offset, rows):

        @pl.when(came & (shard >= other * n_half) & (shard < (other + 1) * n_half))
        def _():
            out_ref[span((shard - other * n_half) * rows, rows), :] = ref[...]


def other_half(line, n_half, offset, rows, dep):
    keep = line[0].shape[1]
    return call(
        functools.partial(half_kernel, n_half, offset, rows),
        "half_for_other_core",
        shape((n_half * rows, keep), BF16),
        [VMEM] * len(line) + [ANY],
        (*line, dep),
        out_specs=VMEM,
    )


def weight_kernel(n_half, n_row, offset, cot_ref, cot_other_ref, other_ref, *refs):
    count = len(refs) - n_row - 3
    line, own_ref, send_refs = refs[:count], refs[count + 1], refs[count + 2 : count + 1 + n_row]
    mine_ref, total_ref = refs[-2:]
    dp, row = lax.axis_index("dp"), lax.axis_index("row")
    rows = mine_ref.shape[0] // n_half
    for came, shard, ref in each_shard(line, offset, rows):

        @pl.when(came & (shard >= dp * n_half) & (shard < (dp + 1) * n_half))
        def _():
            mine_ref[span((shard - dp * n_half) * rows, rows), :] = ref[...]

    sub = own_ref.shape[0]
    bound = jnp.zeros((8, 128), F32)
    for step in range(n_row):
        rows = span((row ^ step) * sub, sub)
        value = dot(mine_ref[rows, :], cot_ref[...], 1, 1) + dot(other_ref[rows, :], cot_other_ref[...], 1, 1)
        if step == 0:
            own_ref[...] = value
        else:
            total_ref[step - 1] = value
            bound = jnp.maximum(bound, tile_max(value))
    for step in range(1, n_row):
        write_payload(
            send_refs[step - 1],
            lambda first, size, step=step: total_ref[step - 1, span(first, size), :],
            bound,
        )


def weight_partial(cot, cot_other, other, line, n_half, n_row, offset, dep):
    half, keep = other.shape
    heads = cot.shape[0]
    sub = half // n_row
    return call(
        functools.partial(weight_kernel, n_half, n_row, offset),
        "grad_weight_partial",
        [shape((sub, heads), F32)] + [shape((sub + HEADER, heads), BF16)] * (n_row - 1),
        [VMEM] * (3 + len(line)) + [ANY],
        (cot, cot_other, other, *line, dep),
        scratch=[pltpu.VMEM((half, keep), BF16), pltpu.VMEM((n_row - 1, sub, heads), F32)],
        flops=4 * half * keep * heads,
        mib=20,
    )


def weight_last_kernel(n_came, start, own_ref, *refs):
    came_refs, (out_ref, total_ref, sem) = refs[:n_came], refs[-3:]
    sub = own_ref.shape[0]
    undo = [read_header(came)[0] for came in came_refs]
    size = 16
    steps = sub // size
    copies = []
    for first, last in ((0, steps // 2), (steps // 2, steps)):

        @pl.loop(first, last)
        def _(i):
            rows = span(i * size, size)
            total = own_ref[rows, :]
            for came, scale in zip(came_refs, undo):
                total = total + root(came[rows, :], scale)
            total_ref[rows, :] = total

        rows = pl.ds(first * size, (last - first) * size)
        target = out_ref.at[pl.ds(start + first * size, (last - first) * size), :]
        copies.append(pltpu.make_async_copy(total_ref.at[rows, :], target, sem.at[len(copies)]))
        copies[-1].start()
    for copy in copies:
        copy.wait()


def weight_last(own, came, base, dep, start, w_rows):
    sub, heads = own.shape
    return call(
        functools.partial(weight_last_kernel, len(came), start),
        "grad_weight_last",
        shape((w_rows, heads), F32),
        [VMEM] * (1 + len(came)) + [ANY] * 2,
        (own, *came, base, dep),
        out_specs=ANY,
        scratch=[pltpu.VMEM((sub, heads), F32), pltpu.SemaphoreType.DMA((2,))],
        aliases={1 + len(came): 0} if start else None,
        flops=20 * sub * heads * len(came),
    )


def query_kernel(sizes, blocks, n_half, *refs):
    parts = len(sizes)
    w_refs = refs[: 2 * parts]
    out_ref, tile_ref, sem, *panels = refs[-3 - parts :]
    pieces = refs[2 * parts : -4 - parts]
    middle, outer = pieces[:3], pieces[3:]
    per_part = len(outer) // parts
    dp = lax.axis_index("dp")
    for p, (_, _, offset, rows) in enumerate(part_rows(sizes, blocks)):
        mine = outer[p * per_part : (p + 1) * per_part]
        line = mine[: per_part // 2] + middle + mine[per_part // 2 :]
        for came, shard, ref in each_shard(line, offset, rows):

            @pl.when(came)
            def _():
                place = (shard // n_half ^ dp) * n_half + shard % n_half
                panels[p][span(place * rows, rows), :] = ref[...]

    tile = tile_ref.shape[1]
    copies = []
    for i in range(out_ref.shape[0] // tile):
        heads = pl.ds(i * tile, tile)
        total = jnp.zeros(tile_ref.shape[1:], F32)
        for p in range(parts):
            for n in range(2):
                w_ref = w_refs[2 * p + n]
                half = w_ref.shape[0]
                total = total + dot(w_ref[:, heads], panels[p][pl.ds(n * half, half), :], 0, 0)
        tile_ref[i] = total.astype(BF16)
        copies.append(pltpu.make_async_copy(tile_ref.at[i], out_ref.at[heads, :], sem.at[i]))
        copies[-1].start()
    for copy in copies:
        copy.wait()


def all_queries(w_halves, lines, sizes, blocks, n_half, dep):
    heads = w_halves[0].shape[1]
    keep = lines[0][0].shape[1]
    middle = len(lines[0]) // 2
    pieces = lines[0][middle - 1 : middle + 2]
    for line in lines:
        pieces = pieces + line[: middle - 1] + line[middle + 2 :]
    tile = 256
    return call(
        functools.partial(query_kernel, sizes, blocks, n_half),
        "queries",
        shape((heads, keep), BF16),
        [VMEM] * (len(w_halves) + len(pieces)) + [ANY],
        (*w_halves, *pieces, dep),
        out_specs=ANY,
        scratch=[pltpu.VMEM((heads // tile, tile, keep), BF16), pltpu.SemaphoreType.DMA((heads // tile,))]
        + [pltpu.VMEM((2 * w.shape[0], keep), BF16) for w in w_halves[::2]],
        mib=20,
    )


def per_device(tokens, kept_index, w_query, cotangent):
    n_dp, n_row, n_col = (lax.axis_size(a) for a in ("dp", "row", "col"))
    seq_x = tokens[0]
    cot = cotangent[0]
    d_dev, seq_dev = seq_x.shape
    w_rows, heads = w_query.shape
    keep_dev = cot.shape[1]
    drift = keep_dev // 4
    sizes = part_sizes(w_rows)
    parts = len(sizes)
    blocks = d_dev // w_rows
    n_half = n_col // n_dp
    layout = list(part_rows(sizes, blocks))

    def to_row(value, step):
        return lax.ppermute(value, "row", [(r, r ^ step) for r in range(n_row)])

    def to_core(value):
        return lax.ppermute(value, "dp", [(i, i ^ 1) for i in range(n_dp)])

    def along(value, sources, step):
        return lax.ppermute(value, "col", [(c, c + step) for c in sources])

    leaving, rows = call(
        functools.partial(pick_leaving_kernel, blocks, sizes, n_row, keep_dev),
        "pick_leaving",
        [shape((d_dev, drift), BF16), shape((d_dev, seq_dev), BF16)],
        [VMEM, ANY],
        (kept_index, seq_x),
        scratch=[pltpu.VMEM((seq_dev, drift), BF16), pltpu.SemaphoreType.DMA((blocks,))],
        mib=40,
    )
    arrived = lax.ppermute(leaving, "row", [(r, r + 1) for r in range(n_row - 1)])
    picked = call(
        functools.partial(pick_own_kernel, blocks, sizes),
        "pick_own",
        shape((d_dev, keep_dev), BF16),
        [VMEM] * 2,
        (kept_index, rows),
        out_specs=VMEM,
        scratch=[pltpu.VMEM((seq_dev, keep_dev), BF16)],
    )
    kept = call(
        add_arrived_kernel,
        "add_arrived",
        shape((d_dev, keep_dev), BF16),
        [VMEM] * 2,
        (arrived, picked),
        out_specs=VMEM,
        aliases={1: 0},
    )

    own_w = list(
        call(
            functools.partial(split_kernel, sizes),
            "split_rows",
            [shape((size, heads), BF16) for size in sizes],
            [ANY, ANY],
            (w_query, leaving),
            scratch=[pltpu.SemaphoreType.DMA((parts,))],
        )
    )
    mine, other = [], []
    for p in range(parts):
        if p > 0:
            (own_w[p],) = after([own_w[p]], mine[-1:])
        pieces = [own_w[p]] + [to_row(own_w[p], step) for step in range(1, n_row)]
        mine.append(collect(pieces))
        other.append(to_core(mine[p]))

    owns, cames = [None] * parts, [None] * parts
    right = [[along(kept, range(n_col - 1), 1)] for _ in range(parts)]
    left = [[along(kept, range(1, n_col), -1)] for _ in range(parts)]
    for p in range(1, parts):
        right[p][0], left[p][0] = right[0][0], left[0][0]
    token = kept

    def line_of(p):
        return right[p][n_col - 2 :: -1] + [kept] + left[p][: n_col - 1]

    def step(p, t):
        nonlocal token
        offset = layout[p][2] if t == 1 else 0
        out_r, out_l = line_step(
            n_col, n_half, t, offset, layout[p][3], mine[p], other[p], cot, right[p][-1], left[p][-1], token
        )
        token = out_r
        right[p].append(along(out_r, range(n_col - 1), 1))
        left[p].append(along(out_l, range(1, n_col), -1))

    def give(p):
        nonlocal token
        token = other_half(line_of(p), n_half, layout[p][2], layout[p][3], token)
        return to_core(token)

    def weigh(p, theirs):
        nonlocal token
        owns[p], *sends = weight_partial(
            cot, cot_other, theirs, line_of(p), n_half, n_row, layout[p][2], token
        )
        token = owns[p]
        cames[p] = [to_row(send, step) for step, send in enumerate(sends, 1)]

    grad_kept, grad_weight = leaving, leaving

    def finish_kept(p):
        nonlocal grad_kept, token
        start, size = layout[p][:2]
        grad_kept = last_sums(
            mine[p], other[p], cot, right[p][-1], left[p][-1], grad_kept, token, start, size, blocks, n_half, d_dev
        )
        token = grad_kept

    def finish_weight(p):
        nonlocal grad_weight, token
        grad_weight = weight_last(owns[p], cames[p], grad_weight, token, layout[p][0], w_rows)
        token = grad_weight

    step(0, 1)
    (cot_for_core,) = after([cot], [token])
    cot_other = to_core(cot_for_core)
    if parts == 1:
        for t in range(2, n_col):
            step(0, t)
        weigh(0, give(0))
    else:
        for t in range(2, n_col):
            step(1, t - 1)
            step(0, t)
            if t == n_col - 1:
                theirs = give(0)
        weigh(0, theirs)
        theirs = give(1)
        step(1, n_col - 1)
        weigh(1, theirs)
    queries = all_queries(
        [h for p in range(parts) for h in (mine[p], other[p])],
        [line_of(p) for p in range(parts)],
        sizes,
        blocks,
        n_half,
        token,
    )
    token = queries
    for p in range(parts):
        finish_kept(p)
        finish_weight(p)
    return (queries[None], grad_kept[None], grad_weight)


def part_sizes(w_rows):
    return (w_rows // 2, w_rows // 2) if w_rows % 32 == 0 else (w_rows,)


def solution(mesh):
    in_specs = (
        P("dp", "col", "row"),
        P("dp", None),
        P(("dp", "row"), "col"),
        P("dp", "col", "row"),
    )
    out_specs = (P("dp", "col", "row"), P("dp", "col", "row"), P(("dp", "row"), "col"))
    return jax.shard_map(
        per_device, mesh=mesh, in_specs=in_specs, out_specs=out_specs, check_vma=False
    )
```

```python
import functools

import jax
import jax.numpy as jnp
from jax import lax
from jax.experimental import pallas as pl
from jax.experimental.pallas import tpu as pltpu
from jax.sharding import PartitionSpec as P

HEADER = 16
OFFSET = 128.0
F32 = jnp.float32
BF16 = jnp.bfloat16
ANY = pl.BlockSpec(memory_space=pl.ANY)
VMEM = pl.BlockSpec(memory_space=pltpu.VMEM)
HBM = pl.BlockSpec(memory_space=pltpu.HBM)


def call(kernel, name, out_shape, in_specs, args, out_specs=None, scratch=(), aliases=None, flops=0, mib=14):
    moved = sum(a.size * a.dtype.itemsize for a, s in zip(args, in_specs) if s is VMEM)
    return pl.pallas_call(
        kernel,
        out_shape=out_shape,
        in_specs=in_specs,
        out_specs=out_specs if out_specs is not None else [VMEM] * len(out_shape),
        scratch_shapes=scratch,
        input_output_aliases=aliases or {},
        compiler_params=pltpu.CompilerParams(vmem_limit_bytes=mib * 2**20),
        cost_estimate=pl.CostEstimate(flops=1, bytes_accessed=1, transcendentals=0),
        name=name,
    )(*args)


def shape(dims, dtype):
    return jax.ShapeDtypeStruct(dims, dtype)


TOKEN = shape((8, 128), F32)


def dot(a, b, ca, cb):
    return lax.dot_general(a, b, (((ca,), (cb,)), ((), ())), preferred_element_type=F32)


def span(start, size):
    return pl.ds(pl.multiple_of(start, 16), size)


def chunks(rows):
    size = 32 if rows % 32 == 0 else 16
    return size, rows // size


def exponent(bound):
    return jnp.clip(jnp.floor(14.99 - jnp.log2(jnp.maximum(bound, 1e-30))), -100.0, 100.0)


def power(values, scale):
    v = values * scale
    square = v * v
    fourth = square * square
    return (fourth * square * (v * jnp.abs(v))).astype(BF16)


def root(code, scale):
    y = code.astype(F32)
    quarter = lax.rsqrt(lax.rsqrt(jnp.maximum(jnp.abs(y), 1e-37)))
    size = quarter * lax.rsqrt(quarter) * scale
    return jnp.where(y > 0.0, size, jnp.where(y < 0.0, -size, 0.0))


def tile_max(values):
    most = jnp.max(jnp.abs(values), axis=0, keepdims=True)
    return jnp.broadcast_to(jnp.max(most, axis=1, keepdims=True), (8, 128))


def write_header(out_ref, expo):
    rows = out_ref.shape[0] - HEADER
    code = jnp.broadcast_to((expo + OFFSET)[0:1, 0:1], (HEADER, out_ref.shape[1]))
    out_ref[rows:, :] = code.astype(BF16)


def write_payload(out_ref, value_of, bound):
    expo = exponent(bound)
    scale = jnp.exp2(expo)[0:1, 0:1]
    size, count = chunks(out_ref.shape[0] - HEADER)

    @pl.loop(0, count)
    def _(i):
        out_ref[span(i * size, size), :] = power(value_of(i * size, size), scale)

    write_header(out_ref, expo)


def read_header(came_ref):
    rows = came_ref.shape[0] - HEADER
    code = came_ref[rows:, :][0:8, 0:128].astype(F32)
    came = code > 0.0
    expo = jnp.where(came, code - OFFSET, 0.0)
    return jnp.exp2(-expo)[0:1, 0:1], jnp.where(came, jnp.exp2(15.0 - expo), 0.0)


def part_rows(sizes, blocks):
    start = 0
    for size in sizes:
        yield start, size, start * blocks, size * blocks
        start += size


def onehot_of(index_ref, first, count, seq_dev):
    index = index_ref[:, pl.ds(pl.multiple_of(first, 128), count)] - lax.axis_index("row") * seq_dev
    positions = lax.broadcasted_iota(jnp.int32, (seq_dev, count), 0)
    return (positions == index).astype(F32).astype(BF16)


def pick_leaving_kernel(blocks, sizes, n_row, keep_dev, index_ref, x_ref, leaving_ref, rows_ref, onehot_ref, sem):
    d_dev, seq_dev = rows_ref.shape
    step = d_dev // blocks

    def copy(b):
        rows = pl.ds(b * step, step)
        return pltpu.make_async_copy(x_ref.at[rows, :], rows_ref.at[rows, :], sem.at[b])

    for b in range(blocks):
        copy(b).start()
    after = jnp.minimum(lax.axis_index("row") + 1, n_row - 1) * keep_dev
    onehot_ref[...] = onehot_of(index_ref, after, leaving_ref.shape[1], seq_dev)
    for b in range(blocks):
        copy(b).wait()
        for start, size, offset, _ in part_rows(sizes, blocks):
            picked = dot(rows_ref[pl.ds(b * step + start, size), :], onehot_ref[...], 1, 0)
            leaving_ref[pl.ds(offset + b * size, size), :] = picked.astype(BF16)


def pick_own_kernel(blocks, sizes, index_ref, rows_ref, kept_ref, onehot_ref):
    d_dev, seq_dev = rows_ref.shape
    keep_dev = kept_ref.shape[1]
    onehot_ref[...] = onehot_of(index_ref, lax.axis_index("row") * keep_dev, keep_dev, seq_dev)
    for b in range(blocks):
        for start, size, offset, _ in part_rows(sizes, blocks):
            picked = dot(rows_ref[pl.ds(b * (d_dev // blocks) + start, size), :], onehot_ref[...], 1, 0)
            kept_ref[pl.ds(offset + b * size, size), :] = picked.astype(BF16)


def add_arrived_kernel(arrived_ref, in_ref, dep_ref, out_ref):
    drift = arrived_ref.shape[1]
    out_ref[:, :drift] = in_ref[:, :drift] + arrived_ref[...]


def nothing_kernel(*refs):
    pass


def after(values, deps):
    return call(
        nothing_kernel,
        "after",
        [shape(v.shape, v.dtype) for v in values],
        [ANY] * (len(values) + len(deps)),
        (*values, *deps),
        out_specs=[ANY] * len(values),
        aliases={i: i for i in range(len(values))},
        mib=1,
    )


def split_kernel(sizes, w_ref, *refs):
    out_refs, sem = refs[:-1], refs[-1]
    copies = [
        pltpu.make_async_copy(w_ref.at[pl.ds(start, size), :], out_refs[p], sem.at[p])
        for p, (start, size, _, _) in enumerate(part_rows(sizes, 1))
    ]
    for copy in copies:
        copy.start()
    for copy in copies:
        copy.wait()


def join_kernel(*refs):
    count = len(refs) // 3
    for n in range(count):
        top, bottom, out_ref = refs[2 * n], refs[2 * n + 1], refs[2 * count + n]
        rows = top.shape[0]
        out_ref[:rows, :] = top[...]
        out_ref[rows:, :] = bottom[...]


def join(pairs):
    arrays = [array for pair in pairs for array in pair]
    return call(
        join_kernel,
        "join_rows",
        [shape((a.shape[0] + b.shape[0], a.shape[1]), a.dtype) for a, b in pairs],
        [VMEM] * len(arrays),
        arrays,
    )


def collect_kernel(plan, *refs):
    out_refs = refs[-len(plan) :]
    row = lax.axis_index("row")
    for out_ref, sources in zip(out_refs, plan):
        size = out_ref.shape[0] // len(sources)
        for step, piece, first in sources:
            out_ref[span((row ^ step) * size, size), :] = refs[piece][pl.ds(first, size), :]


def collect(pieces, plan, sizes, deps):
    heads = pieces[0].shape[1]
    return call(
        functools.partial(collect_kernel, plan),
        "collect_rows",
        [shape((len(sources) * size, heads), BF16) for sources, size in zip(plan, sizes)],
        [VMEM] * len(pieces) + [ANY] * len(deps),
        (*pieces, *deps),
    )


def copy_rows(out_ref, from_ref, first):
    size, count = chunks(out_ref.shape[0])

    @pl.loop(0, count)
    def _(i):
        out_ref[span(i * size, size), :] = from_ref[span(first + i * size, size), :]


def partial_into(out_ref, block, n_half, mine_ref, other_ref, cot_ref, rows_ref):
    shard = out_ref.shape[0]
    first = (block % n_half) * shard
    here = block // n_half == lax.axis_index("dp")
    pl.when(here)(lambda: copy_rows(rows_ref, mine_ref, first))
    pl.when(jnp.logical_not(here))(lambda: copy_rows(rows_ref, other_ref, first))
    out_ref[...] = dot(rows_ref[...], cot_ref[...], 1, 0)


def step_kernel(
    n_col, n_half, t, offset, mine_ref, other_ref, cot_ref, came_r, came_l, dep_ref, out_r, out_l, term_ref, rows_ref
):
    shard = out_r.shape[0] - HEADER
    col = lax.axis_index("col")

    @pl.loop(0, 2)
    def _(way):
        place = jnp.where(way == 0, col, n_col - 1 - col)

        @pl.when(place < t)
        def _():
            block = jnp.where(way == 0, n_col - t + col, t - n_col + col)
            partial_into(term_ref.at[way], block, n_half, mine_ref, other_ref, cot_ref, rows_ref)

    for way, (place, came, out) in enumerate(((col, came_r, out_r), (n_col - 1 - col, came_l, out_l))):
        pl.when(place >= t)(lambda: copy_rows(out.at[pl.ds(0, shard), :], came, offset))

        @pl.when(place < t)
        def _():
            bound = tile_max(term_ref[way])
            if t == 1:
                write_payload(out, lambda first, size: term_ref[way, span(first, size), :], bound)
            else:
                undo, came_bound = read_header(came)

                def total(first, size):
                    rows = span(first, size)
                    return term_ref[way, rows, :] + root(came[rows, :], undo)

                write_payload(out, total, bound + came_bound)


def line_step(n_col, n_half, t, offset, shard, mine, other, cot, came_r, came_l, dep):
    keep = cot.shape[1]
    payload = shape((shard + HEADER, keep), BF16)
    return call(
        functools.partial(step_kernel, n_col, n_half, t, offset),
        "line_step",
        [payload, payload],
        [VMEM] * 5 + [ANY],
        (mine, other, cot, came_r, came_l, dep),
        scratch=[pltpu.VMEM((2, shard, keep), F32), pltpu.VMEM((shard, cot.shape[0]), BF16)],
    )


def last_kernel(
    start, size, blocks, n_half, mine_ref, other_ref, cot_ref, r_ref, l_ref, base_ref, dep_ref, out_ref, *rest
):
    done_ref, total_ref, rows_ref, sem = rest
    done_ref[...] = jnp.zeros_like(done_ref)
    step = out_ref.shape[0] // blocks
    partial_into(total_ref, lax.axis_index("col"), n_half, mine_ref, other_ref, cot_ref, rows_ref)
    undo_r, _ = read_header(r_ref)
    undo_l, _ = read_header(l_ref)
    few, count = chunks(size)
    copies = []
    for b in range(blocks):

        @pl.loop(0, count)
        def _(i):
            rows = span(b * size + i * few, few)
            came = root(r_ref[rows, :], undo_r) + root(l_ref[rows, :], undo_l)
            total_ref[rows, :] = total_ref[rows, :] + came

        target = out_ref.at[pl.ds(b * step + start, size), :]
        copies.append(pltpu.make_async_copy(total_ref.at[pl.ds(b * size, size), :], target, sem.at[b]))
        copies[-1].start()
    for copy in copies:
        copy.wait()


def last_sums(mine, other, cot, came_r, came_l, base, dep, start, size, blocks, n_half, d_dev):
    shard, keep = came_r.shape[0] - HEADER, came_r.shape[1]
    return call(
        functools.partial(last_kernel, start, size, blocks, n_half),
        "grad_kept_last",
        [shape((d_dev, keep), F32), TOKEN],
        [VMEM] * 5 + [HBM if start else ANY, ANY],
        (mine, other, cot, came_r, came_l, base, dep),
        out_specs=[HBM, VMEM],
        scratch=[
            pltpu.VMEM((shard, keep), F32),
            pltpu.VMEM((shard, cot.shape[0]), BF16),
            pltpu.SemaphoreType.DMA((blocks,)),
        ],
        aliases={5: 0} if start else None,
    )


def each_shard(line, offset, rows):
    n_col = lax.axis_size("col")
    col = lax.axis_index("col")
    for n, ref in enumerate(line):
        away = n - len(line) // 2
        shard = col + away
        whole = abs(away) < 2
        yield (shard >= 0) & (shard < n_col), shard, ref.at[pl.ds(offset if whole else 0, rows), :]


def early(dp, n_half):
    return lax.axis_index("col") // n_half == dp


def wanted(when, dp, n_half):
    return None if when is None else early(dp, n_half) == when


def run_if(condition, body):
    if condition is None:
        body()
    else:
        pl.when(condition)(body)


def copy_half(dp, n_half, lines, layout, out_ref):
    base = 0
    for line, (_, _, offset, rows) in zip(lines, layout):
        for came, shard, ref in each_shard(line, offset, rows):

            @pl.when(came & (shard // n_half == dp))
            def _():
                out_ref[span(base + (shard % n_half) * rows, rows), :] = ref[...]

        base += n_half * rows


def half_kernel(n_half, layout, when, *refs):
    arrays, out_ref = refs[:-2], refs[-1]
    other = 1 - lax.axis_index("dp")
    run_if(
        wanted(when, other, n_half),
        lambda: copy_half(other, n_half, split_lines(arrays, len(layout)), layout, out_ref),
    )


def split_lines(arrays, parts):
    count = len(arrays) // parts
    return [arrays[p * count : (p + 1) * count] for p in range(parts)]


def other_half(lines, layout, n_half, when, dep):
    keep = lines[0][0].shape[1]
    arrays = [array for line in lines for array in line]
    return call(
        functools.partial(half_kernel, n_half, layout, when),
        "half_for_other_core",
        shape((n_half * sum(rows for _, _, _, rows in layout), keep), BF16),
        [VMEM] * len(arrays) + [ANY],
        (*arrays, dep),
        out_specs=VMEM,
    )


DIRECT, SQUARE = "direct", "square"


def weight_kernel(n_half, n_row, layout, when, form, count, cot_ref, cot_other_ref, other_ref, *refs):
    arrays, own_ref, send_refs = refs[:count], refs[count + 1], refs[count + 2 : -2]
    mine_ref, total_ref = refs[-2:]
    dp, row = lax.axis_index("dp"), lax.axis_index("row")
    sub = own_ref.shape[0]
    apart = (2,) if form == SQUARE else ()

    def body():
        copy_half(dp, n_half, split_lines(arrays, len(layout)), layout, mine_ref)
        base = start = 0
        for _, size, _, rows in layout:

            @pl.loop(0, n_row)
            def _(step):
                at = span(base + (row ^ step) * size, size)
                value = dot(mine_ref[at, :], cot_ref[...], 1, 1) + dot(other_ref[at, :], cot_other_ref[...], 1, 1)
                target = pl.ds(start, size)

                @pl.when(step == 0)
                def _():
                    own_ref[target, :] = value

                @pl.when(step > 0)
                def _():
                    total_ref[step - 1, target, :] = value

            start += size
            base += n_half * rows
        bound = tile_max(total_ref[0])
        for step in range(2, n_row):
            if step not in apart:
                bound = jnp.maximum(bound, tile_max(total_ref[step - 1]))
        for step in apart:
            send_refs[1][...] = total_ref[step - 1]
        if form == SQUARE:
            expo = exponent(bound)
            scale = jnp.exp2(expo)[0:1, 0:1]
            size, count = chunks(sub)
            for n, step in enumerate((1, 3)):

                @pl.loop(0, count)
                def _(i):
                    value = total_ref[step - 1, span(i * size, size), :]
                    send_refs[0][span(n * sub + i * size, size), :] = power(value, scale)

            write_header(send_refs[0], expo)
        else:
            for n, send_ref in enumerate(send_refs):
                write_payload(send_ref, lambda first, size: total_ref[n, span(first, size), :], bound)

    run_if(wanted(when, dp, n_half), body)


def weight_partial(cot, cot_other, other, lines, layout, n_half, n_row, when, form, dep):
    half, keep = other.shape
    heads = cot.shape[0]
    sub = sum(size for _, size, _, _ in layout)
    arrays = [array for line in lines for array in line]
    if form == SQUARE:
        outputs = [shape((2 * sub + HEADER, heads), BF16), shape((sub, heads), F32)]
    else:
        outputs = [shape((sub + HEADER, heads), BF16)] * (n_row - 1)
    return call(
        functools.partial(weight_kernel, n_half, n_row, layout, when, form, len(arrays)),
        "grad_weight_partial",
        [shape((sub, heads), F32)] + outputs,
        [VMEM] * (3 + len(arrays)) + [ANY],
        (cot, cot_other, other, *arrays, dep),
        scratch=[pltpu.VMEM((half, keep), BF16), pltpu.VMEM((n_row - 1, sub, heads), F32)],
        mib=24,
    )


def weight_middle_kernel(n_half, when, kept_ref, came_ref, dep_ref, out_ref):
    sub = kept_ref.shape[0]

    def body():
        undo, bound = read_header(came_ref)

        def total(first, size):
            return kept_ref[span(first, size), :] + root(came_ref[span(sub + first, size), :], undo)

        write_payload(out_ref, total, bound + tile_max(kept_ref[...]))

    run_if(wanted(when, lax.axis_index("dp"), n_half), body)


def weight_middle(kept, came, n_half, when, dep):
    sub, heads = kept.shape
    return call(
        functools.partial(weight_middle_kernel, n_half, when),
        "grad_weight_middle",
        shape((sub + HEADER, heads), BF16),
        [VMEM] * 2 + [ANY],
        (kept, came, dep),
        out_specs=VMEM,
    )


def weight_last_kernel(n_came, start, n_half, when, own_ref, *refs):
    came_refs, (out_ref, done_ref, total_ref, sem) = refs[:n_came], refs[-4:]
    sub = own_ref.shape[0]
    done_ref[...] = jnp.zeros_like(done_ref)

    def body():
        undo = [read_header(came)[0] for came in came_refs]
        size = 16
        steps = sub // size
        copies = []
        for first, last in ((0, steps // 2), (steps // 2, steps)):

            @pl.loop(first, last)
            def _(i):
                rows = span(i * size, size)
                total = own_ref[rows, :]
                for came, scale in zip(came_refs, undo):
                    total = total + root(came[rows, :], scale)
                total_ref[rows, :] = total

            rows = pl.ds(first * size, (last - first) * size)
            target = out_ref.at[pl.ds(start + first * size, (last - first) * size), :]
            copies.append(pltpu.make_async_copy(total_ref.at[rows, :], target, sem.at[len(copies)]))
            copies[-1].start()
        for copy in copies:
            copy.wait()

    run_if(wanted(when, lax.axis_index("dp"), n_half), body)


def weight_last(own, came, base, dep, start, w_rows, n_half, when):
    sub, heads = own.shape
    again = base.shape == (w_rows, heads) and base.dtype == F32
    return call(
        functools.partial(weight_last_kernel, len(came), start, n_half, when),
        "grad_weight_last",
        [shape((w_rows, heads), F32), TOKEN],
        [VMEM] * (1 + len(came)) + [HBM if again else ANY, ANY],
        (own, *came, base, dep),
        out_specs=[HBM, VMEM],
        scratch=[pltpu.VMEM((sub, heads), F32), pltpu.SemaphoreType.DMA((2,))],
        aliases={1 + len(came): 0} if again else None,
    )


def query_kernel(sizes, blocks, n_half, *refs):
    parts = len(sizes)
    w_refs = refs[: 2 * parts]
    out_ref, done_ref, tile_ref, sem, *panels = refs[-4 - parts :]
    done_ref[...] = jnp.zeros_like(done_ref)
    pieces = refs[2 * parts : -5 - parts]
    middle, outer = pieces[:3], pieces[3:]
    per_part = len(outer) // parts
    dp = lax.axis_index("dp")
    for p, (_, _, offset, rows) in enumerate(part_rows(sizes, blocks)):
        mine = outer[p * per_part : (p + 1) * per_part]
        line = mine[: per_part // 2] + middle + mine[per_part // 2 :]
        for came, shard, ref in each_shard(line, offset, rows):

            @pl.when(came)
            def _():
                place = (shard // n_half ^ dp) * n_half + shard % n_half
                panels[p][span(place * rows, rows), :] = ref[...]

    tile = tile_ref.shape[1]

    def copy(i):
        return pltpu.make_async_copy(tile_ref.at[i], out_ref.at[span(i * tile, tile), :], sem.at[i])

    count = out_ref.shape[0] // tile

    @pl.loop(0, count)
    def _(i):
        heads = pl.ds(pl.multiple_of(i * tile, tile), tile)
        total = jnp.zeros(tile_ref.shape[1:], F32)
        for p in range(parts):
            for n in range(2):
                w_ref = w_refs[2 * p + n]
                half = w_ref.shape[0]
                total = total + dot(w_ref[:, heads], panels[p][pl.ds(n * half, half), :], 0, 0)
        tile_ref[i] = total.astype(BF16)
        copy(i).start()

    for i in range(count):
        copy(i).wait()


def all_queries(w_halves, lines, sizes, blocks, n_half, dep):
    heads = w_halves[0].shape[1]
    keep = lines[0][0].shape[1]
    middle = len(lines[0]) // 2
    pieces = lines[0][middle - 1 : middle + 2]
    for line in lines:
        pieces = pieces + line[: middle - 1] + line[middle + 2 :]
    tile = 256
    return call(
        functools.partial(query_kernel, sizes, blocks, n_half),
        "queries",
        [shape((heads, keep), BF16), TOKEN],
        [VMEM] * (len(w_halves) + len(pieces)) + [ANY],
        (*w_halves, *pieces, dep),
        out_specs=[HBM, VMEM],
        scratch=[pltpu.VMEM((heads // tile, tile, keep), BF16), pltpu.SemaphoreType.DMA((heads // tile,))]
        + [pltpu.VMEM((2 * w.shape[0], keep), BF16) for w in w_halves[::2]],
        mib=20,
    )


def per_device(tokens, kept_index, w_query, cotangent):
    n_dp, n_row, n_col = (lax.axis_size(a) for a in ("dp", "row", "col"))
    seq_x = tokens[0]
    cot = cotangent[0]
    d_dev, seq_dev = seq_x.shape
    w_rows, heads = w_query.shape
    keep_dev = cot.shape[1]
    drift = keep_dev // 4
    sizes = part_sizes(w_rows)
    parts = len(sizes)
    blocks = d_dev // w_rows
    n_half = n_col // n_dp
    layout = list(part_rows(sizes, blocks))

    def to_row(value, step):
        return lax.ppermute(value, "row", [(r, r ^ step) for r in range(n_row)])

    def to_core(value):
        return lax.ppermute(value, "dp", [(i, i ^ 1) for i in range(n_dp)])

    def along(value, sources, step):
        return lax.ppermute(value, "col", [(c, c + step) for c in sources])

    if parts == 2 and n_row == 4:
        own_w = call(
            functools.partial(split_kernel, sizes),
            "split_rows",
            [shape((size, heads), BF16) for size in sizes],
            [HBM],
            (w_query,),
            scratch=[pltpu.SemaphoreType.DMA((parts,))],
        )
        ways = ((1, 2), (2, 1))
        pieces = join([(w, to_row(w, one)) for w, (one, _) in zip(own_w, ways)])
        pieces = [*pieces] + [to_row(pair, two) for pair, (_, two) in zip(pieces, ways)]
        plan = [
            ((0, p, 0), (one, p, size), (two, p + 2, 0), (3, p + 2, size))
            for p, ((one, two), size) in enumerate(zip(ways, sizes))
        ]
    else:
        pieces = [w_query] + [to_row(w_query, step) for step in range(1, n_row)]
        plan = [tuple((step, step, start) for step in range(n_row)) for start, _, _, _ in layout]

    leaving, rows = call(
        functools.partial(pick_leaving_kernel, blocks, sizes, n_row, keep_dev),
        "pick_leaving",
        [shape((d_dev, drift), BF16), shape((d_dev, seq_dev), BF16)],
        [VMEM, ANY],
        (kept_index, seq_x),
        scratch=[pltpu.VMEM((seq_dev, drift), BF16), pltpu.SemaphoreType.DMA((blocks,))],
        mib=40,
    )
    arrived = lax.ppermute(leaving, "row", [(r, r + 1) for r in range(n_row - 1)])
    cot_other = to_core(cot)
    picked = call(
        functools.partial(pick_own_kernel, blocks, sizes),
        "pick_own",
        shape((d_dev, keep_dev), BF16),
        [VMEM] * 2,
        (kept_index, rows),
        out_specs=VMEM,
        scratch=[pltpu.VMEM((seq_dev, keep_dev), BF16)],
    )
    kept = call(
        add_arrived_kernel,
        "add_arrived",
        shape((d_dev, keep_dev), BF16),
        [VMEM] * 2 + [ANY],
        (arrived, picked, cot_other),
        out_specs=VMEM,
        aliases={1: 0},
    )


    right = [[along(kept, range(n_col - 1), 1)] for _ in range(parts)]
    left = [[along(kept, range(1, n_col), -1)] for _ in range(parts)]
    for p in range(1, parts):
        right[p][0], left[p][0] = right[0][0], left[0][0]
    token = kept
    def line_of(p):
        return right[p][n_col - 2 :: -1] + [kept] + left[p][: n_col - 1]

    def step(p, t):
        nonlocal token
        offset = layout[p][2] if t == 1 else 0
        out_r, out_l = line_step(
            n_col, n_half, t, offset, layout[p][3], mine[p], other[p], cot, right[p][-1], left[p][-1], token
        )
        token = out_r
        right[p].append(along(out_r, range(n_col - 1), 1))
        left[p].append(along(out_l, range(1, n_col), -1))

    def device(s, r, c):
        return (s * n_row + r) * n_col + c

    def taking(when):
        return [
            (s, c) for s in range(n_dp) for c in range(n_col) if when is None or (c // n_half == s) == when
        ]

    def give(parts_of, when, lines):
        nonlocal token
        token = other_half(lines, [layout[p] for p in parts_of], n_half, when, token)
        pairs = [((1 - s) * n_col + c, s * n_col + c) for s, c in taking(when)]
        return lax.ppermute(token, ("dp", "col"), pairs)

    def to_rows(send, step, when):
        pairs = [(device(s, r, c), device(s, r ^ step, c)) for s, c in taking(when) for r in range(n_row)]
        return lax.ppermute(send, ("dp", "row", "col"), pairs)

    def weigh(parts_of, when, lines, theirs, form):
        nonlocal token
        own, *sends = weight_partial(
            cot, cot_other, theirs, lines, [layout[p] for p in parts_of], n_half, n_row, when, form, token
        )
        token = own
        return own, sends, layout[parts_of[0]][0], when

    def send_first(own, sends, start, when):
        return own, [to_rows(sends[0], 1, when), sends[1]], start, when

    def send_all(own, sends, start, when):
        return own, [to_rows(send, step, when) for step, send in enumerate(sends, 1)], start, when

    def second(own, came, start, when):
        nonlocal token
        token = weight_middle(came[1], came[0], n_half, when, token)
        return own, [came[0], to_rows(token, 2, when)], start, when

    grad_kept, grad_weight = leaving, leaving

    def finish_kept(p):
        nonlocal grad_kept, token
        start, size = layout[p][:2]
        grad_kept, token = last_sums(
            mine[p], other[p], cot, right[p][-1], left[p][-1], grad_kept, token, start, size, blocks, n_half, d_dev
        )

    def finish_weight(own, came, start, when):
        nonlocal grad_weight, token
        grad_weight, token = weight_last(own, came, grad_weight, token, start, w_rows, n_half, when)

    def collect_all():
        nonlocal token
        shares = collect(pieces, plan, sizes, [token, right[0][0], left[0][0]])
        token = shares[0]
        return shares, [to_core(share) for share in shares]

    def ask():
        nonlocal token
        halves = [h for p in range(parts) for h in (mine[p], other[p])]
        queries, token = all_queries(halves, [line_of(p) for p in range(parts)], sizes, blocks, n_half, token)
        return queries

    every = tuple(range(parts))
    if parts == 2 and n_half == 2 and n_row == 4:
        whole = [right[0][0], kept, left[0][0]]
        theirs = give(every, True, [whole, whole])
        mine, other = collect_all()
        step(0, 1)
        step(1, 1)
        first = send_first(*weigh(every, True, [whole, whole], theirs, SQUARE))
        step(0, 2)
        step(1, 2)
        step(0, 3)
        step(1, 3)
        finish_kept(0)
        theirs = give(every, False, [line_of(p) for p in every])
        first = second(*first)
        queries = ask()
        late = send_all(*weigh(every, False, [line_of(p) for p in every], theirs, DIRECT))
        finish_weight(*first)
        finish_kept(1)
        finish_weight(*late)
    else:
        mine, other = collect_all()
        for t in range(1, n_col):
            for p in every:
                step(p, t)
        theirs = give(every, None, [line_of(p) for p in every])
        late = send_all(*weigh(every, None, [line_of(p) for p in every], theirs, DIRECT))
        queries = ask()
        for p in every:
            finish_kept(p)
        finish_weight(*late)
    return (queries[None], grad_kept[None], grad_weight)


def part_sizes(w_rows):
    return (w_rows // 2, w_rows // 2) if w_rows % 32 == 0 else (w_rows,)


def solution(mesh):
    in_specs = (
        P("dp", "col", "row"),
        P("dp", None),
        P(("dp", "row"), "col"),
        P("dp", "col", "row"),
    )
    out_specs = (P("dp", "col", "row"), P("dp", "col", "row"), P(("dp", "row"), "col"))
    return jax.shard_map(
        per_device, mesh=mesh, in_specs=in_specs, out_specs=out_specs, check_vma=False
    )
```

```python
import functools

import jax
import jax.numpy as jnp
from jax import lax
from jax.experimental import pallas as pl
from jax.experimental.pallas import tpu as pltpu
from jax.sharding import PartitionSpec as P

HEADER = 16
OFFSET = 128.0
F32 = jnp.float32
BF16 = jnp.bfloat16
ANY = pl.BlockSpec(memory_space=pl.ANY)
VMEM = pl.BlockSpec(memory_space=pltpu.VMEM)
HBM = pl.BlockSpec(memory_space=pltpu.HBM)


def call(kernel, name, out_shape, in_specs, args, out_specs=None, scratch=(), aliases=None, flops=0, mib=14):
    moved = sum(a.size * a.dtype.itemsize for a, s in zip(args, in_specs) if s is VMEM)
    return pl.pallas_call(
        kernel,
        out_shape=out_shape,
        in_specs=in_specs,
        out_specs=out_specs if out_specs is not None else [VMEM] * len(out_shape),
        scratch_shapes=scratch,
        input_output_aliases=aliases or {},
        compiler_params=pltpu.CompilerParams(vmem_limit_bytes=mib * 2**20),
        cost_estimate=pl.CostEstimate(flops=1, bytes_accessed=1, transcendentals=0),
        name=name,
    )(*args)


def shape(dims, dtype):
    return jax.ShapeDtypeStruct(dims, dtype)


TOKEN = shape((8, 128), F32)


def dot(a, b, ca, cb):
    return lax.dot_general(a, b, (((ca,), (cb,)), ((), ())), preferred_element_type=F32)


def span(start, size):
    return pl.ds(pl.multiple_of(start, 16), size)


def chunks(rows):
    size = 32 if rows % 32 == 0 else 16
    return size, rows // size


def exponent(bound):
    return jnp.clip(jnp.floor(14.99 - jnp.log2(jnp.maximum(bound, 1e-30))), -100.0, 100.0)


def power(values, scale):
    v = values * scale
    square = v * v
    fourth = square * square
    return (fourth * square * (v * jnp.abs(v))).astype(BF16)


def root(code, scale):
    y = code.astype(F32)
    quarter = lax.rsqrt(lax.rsqrt(jnp.maximum(jnp.abs(y), 1e-37)))
    size = quarter * lax.rsqrt(quarter) * scale
    return jnp.where(y > 0.0, size, jnp.where(y < 0.0, -size, 0.0))


def tile_max(values):
    most = jnp.max(jnp.abs(values), axis=0, keepdims=True)
    return jnp.broadcast_to(jnp.max(most, axis=1, keepdims=True), (8, 128))


def write_header(out_ref, expo):
    rows = out_ref.shape[0] - HEADER
    code = jnp.broadcast_to((expo + OFFSET)[0:1, 0:1], (HEADER, out_ref.shape[1]))
    out_ref[rows:, :] = code.astype(BF16)


def write_payload(out_ref, value_of, bound):
    expo = exponent(bound)
    scale = jnp.exp2(expo)[0:1, 0:1]
    size, count = chunks(out_ref.shape[0] - HEADER)

    @pl.loop(0, count)
    def _(i):
        out_ref[span(i * size, size), :] = power(value_of(i * size, size), scale)

    write_header(out_ref, expo)


def read_header(came_ref):
    rows = came_ref.shape[0] - HEADER
    code = came_ref[rows:, :][0:8, 0:128].astype(F32)
    came = code > 0.0
    expo = jnp.where(came, code - OFFSET, 0.0)
    return jnp.exp2(-expo)[0:1, 0:1], jnp.where(came, jnp.exp2(15.0 - expo), 0.0)


def part_rows(sizes, blocks):
    start = 0
    for size in sizes:
        yield start, size, start * blocks, size * blocks
        start += size


def onehot_of(index_ref, first, count, seq_dev):
    index = index_ref[:, pl.ds(pl.multiple_of(first, 128), count)] - lax.axis_index("row") * seq_dev
    positions = lax.broadcasted_iota(jnp.int32, (seq_dev, count), 0)
    return (positions == index).astype(F32).astype(BF16)


def pick_leaving_kernel(blocks, sizes, n_row, keep_dev, index_ref, x_ref, leaving_ref, rows_ref, onehot_ref, sem):
    d_dev, seq_dev = rows_ref.shape
    step = d_dev // blocks

    def copy(b):
        rows = pl.ds(b * step, step)
        return pltpu.make_async_copy(x_ref.at[rows, :], rows_ref.at[rows, :], sem.at[b])

    for b in range(blocks):
        copy(b).start()
    after = jnp.minimum(lax.axis_index("row") + 1, n_row - 1) * keep_dev
    onehot_ref[...] = onehot_of(index_ref, after, leaving_ref.shape[1], seq_dev)
    for b in range(blocks):
        copy(b).wait()
        for start, size, offset, _ in part_rows(sizes, blocks):
            picked = dot(rows_ref[pl.ds(b * step + start, size), :], onehot_ref[...], 1, 0)
            leaving_ref[pl.ds(offset + b * size, size), :] = picked.astype(BF16)


def pick_own_kernel(blocks, sizes, index_ref, rows_ref, kept_ref, onehot_ref):
    d_dev, seq_dev = rows_ref.shape
    keep_dev = kept_ref.shape[1]
    onehot_ref[...] = onehot_of(index_ref, lax.axis_index("row") * keep_dev, keep_dev, seq_dev)
    for b in range(blocks):
        for start, size, offset, _ in part_rows(sizes, blocks):
            picked = dot(rows_ref[pl.ds(b * (d_dev // blocks) + start, size), :], onehot_ref[...], 1, 0)
            kept_ref[pl.ds(offset + b * size, size), :] = picked.astype(BF16)


def add_arrived_kernel(arrived_ref, in_ref, dep_ref, out_ref):
    drift = arrived_ref.shape[1]
    out_ref[:, :drift] = in_ref[:, :drift] + arrived_ref[...]


def nothing_kernel(*refs):
    pass


def after(values, deps):
    return call(
        nothing_kernel,
        "after",
        [shape(v.shape, v.dtype) for v in values],
        [ANY] * (len(values) + len(deps)),
        (*values, *deps),
        out_specs=[ANY] * len(values),
        aliases={i: i for i in range(len(values))},
        mib=1,
    )


def split_kernel(sizes, w_ref, *refs):
    out_refs, sem = refs[:-1], refs[-1]
    copies = [
        pltpu.make_async_copy(w_ref.at[pl.ds(start, size), :], out_refs[p], sem.at[p])
        for p, (start, size, _, _) in enumerate(part_rows(sizes, 1))
    ]
    for copy in copies:
        copy.start()
    for copy in copies:
        copy.wait()


def join_kernel(*refs):
    count = len(refs) // 3
    for n in range(count):
        top, bottom, out_ref = refs[2 * n], refs[2 * n + 1], refs[2 * count + n]
        rows = top.shape[0]
        out_ref[:rows, :] = top[...]
        out_ref[rows:, :] = bottom[...]


def join(pairs):
    arrays = [array for pair in pairs for array in pair]
    return call(
        join_kernel,
        "join_rows",
        [shape((a.shape[0] + b.shape[0], a.shape[1]), a.dtype) for a, b in pairs],
        [VMEM] * len(arrays),
        arrays,
    )


def collect_kernel(plan, *refs):
    out_refs = refs[-len(plan) :]
    row = lax.axis_index("row")
    for out_ref, sources in zip(out_refs, plan):
        size = out_ref.shape[0] // len(sources)
        for step, piece, first in sources:
            out_ref[span((row ^ step) * size, size), :] = refs[piece][pl.ds(first, size), :]


def collect(pieces, plan, sizes, deps):
    heads = pieces[0].shape[1]
    return call(
        functools.partial(collect_kernel, plan),
        "collect_rows",
        [shape((len(sources) * size, heads), BF16) for sources, size in zip(plan, sizes)],
        [VMEM] * len(pieces) + [ANY] * len(deps),
        (*pieces, *deps),
    )


def copy_rows(out_ref, from_ref, first):
    size, count = chunks(out_ref.shape[0])

    @pl.loop(0, count)
    def _(i):
        out_ref[span(i * size, size), :] = from_ref[span(first + i * size, size), :]


def partial_into(out_ref, block, n_half, mine_ref, other_ref, cot_ref, rows_ref):
    shard = out_ref.shape[0]
    first = (block % n_half) * shard
    here = block // n_half == lax.axis_index("dp")
    pl.when(here)(lambda: copy_rows(rows_ref, mine_ref, first))
    pl.when(jnp.logical_not(here))(lambda: copy_rows(rows_ref, other_ref, first))
    out_ref[...] = dot(rows_ref[...], cot_ref[...], 1, 0)


def step_kernel(
    n_col, n_half, t, offset, mine_ref, other_ref, cot_ref, came_r, came_l, dep_ref, out_r, out_l, term_ref, rows_ref
):
    shard = out_r.shape[0] - HEADER
    col = lax.axis_index("col")

    @pl.loop(0, 2)
    def _(way):
        place = jnp.where(way == 0, col, n_col - 1 - col)

        @pl.when(place < t)
        def _():
            block = jnp.where(way == 0, n_col - t + col, t - n_col + col)
            partial_into(term_ref.at[way], block, n_half, mine_ref, other_ref, cot_ref, rows_ref)

    for way, (place, came, out) in enumerate(((col, came_r, out_r), (n_col - 1 - col, came_l, out_l))):
        pl.when(place >= t)(lambda: copy_rows(out.at[pl.ds(0, shard), :], came, offset))

        @pl.when(place < t)
        def _():
            bound = tile_max(term_ref[way])
            if t == 1:
                write_payload(out, lambda first, size: term_ref[way, span(first, size), :], bound)
            else:
                undo, came_bound = read_header(came)

                def total(first, size):
                    rows = span(first, size)
                    return term_ref[way, rows, :] + root(came[rows, :], undo)

                write_payload(out, total, bound + came_bound)


def line_step(n_col, n_half, t, offset, shard, mine, other, cot, came_r, came_l, dep):
    keep = cot.shape[1]
    payload = shape((shard + HEADER, keep), BF16)
    return call(
        functools.partial(step_kernel, n_col, n_half, t, offset),
        "line_step",
        [payload, payload],
        [VMEM] * 5 + [ANY],
        (mine, other, cot, came_r, came_l, dep),
        scratch=[pltpu.VMEM((2, shard, keep), F32), pltpu.VMEM((shard, cot.shape[0]), BF16)],
    )


def last_kernel(
    start, size, blocks, n_half, mine_ref, other_ref, cot_ref, r_ref, l_ref, base_ref, dep_ref, out_ref, *rest
):
    done_ref, total_ref, rows_ref, sem = rest
    done_ref[...] = jnp.zeros_like(done_ref)
    step = out_ref.shape[0] // blocks
    partial_into(total_ref, lax.axis_index("col"), n_half, mine_ref, other_ref, cot_ref, rows_ref)
    undo_r, _ = read_header(r_ref)
    undo_l, _ = read_header(l_ref)
    few, count = chunks(size)
    copies = []
    for b in range(blocks):

        @pl.loop(0, count)
        def _(i):
            rows = span(b * size + i * few, few)
            came = root(r_ref[rows, :], undo_r) + root(l_ref[rows, :], undo_l)
            total_ref[rows, :] = total_ref[rows, :] + came

        target = out_ref.at[pl.ds(b * step + start, size), :]
        copies.append(pltpu.make_async_copy(total_ref.at[pl.ds(b * size, size), :], target, sem.at[b]))
        copies[-1].start()
    for copy in copies:
        copy.wait()


def last_sums(mine, other, cot, came_r, came_l, base, dep, start, size, blocks, n_half, d_dev):
    shard, keep = came_r.shape[0] - HEADER, came_r.shape[1]
    return call(
        functools.partial(last_kernel, start, size, blocks, n_half),
        "grad_kept_last",
        [shape((d_dev, keep), F32), TOKEN],
        [VMEM] * 5 + [HBM if start else ANY, ANY],
        (mine, other, cot, came_r, came_l, base, dep),
        out_specs=[HBM, VMEM],
        scratch=[
            pltpu.VMEM((shard, keep), F32),
            pltpu.VMEM((shard, cot.shape[0]), BF16),
            pltpu.SemaphoreType.DMA((blocks,)),
        ],
        aliases={5: 0} if start else None,
    )


def each_shard(line, offset, rows):
    n_col = lax.axis_size("col")
    col = lax.axis_index("col")
    for n, ref in enumerate(line):
        away = n - len(line) // 2
        shard = col + away
        whole = abs(away) < 2
        yield (shard >= 0) & (shard < n_col), shard, ref.at[pl.ds(offset if whole else 0, rows), :]


def early(dp, n_half):
    return lax.axis_index("col") // n_half == dp


def wanted(when, dp, n_half):
    return None if when is None else early(dp, n_half) == when


def run_if(condition, body):
    if condition is None:
        body()
    else:
        pl.when(condition)(body)


def copy_half(dp, n_half, lines, layout, out_ref):
    base = 0
    for line, (_, _, offset, rows) in zip(lines, layout):
        for came, shard, ref in each_shard(line, offset, rows):

            @pl.when(came & (shard // n_half == dp))
            def _():
                out_ref[span(base + (shard % n_half) * rows, rows), :] = ref[...]

        base += n_half * rows


def half_kernel(n_half, layout, when, *refs):
    arrays, out_ref = refs[:-2], refs[-1]
    other = 1 - lax.axis_index("dp")
    run_if(
        wanted(when, other, n_half),
        lambda: copy_half(other, n_half, split_lines(arrays, len(layout)), layout, out_ref),
    )


def split_lines(arrays, parts):
    count = len(arrays) // parts
    return [arrays[p * count : (p + 1) * count] for p in range(parts)]


def other_half(lines, layout, n_half, when, dep):
    keep = lines[0][0].shape[1]
    arrays = [array for line in lines for array in line]
    return call(
        functools.partial(half_kernel, n_half, layout, when),
        "half_for_other_core",
        shape((n_half * sum(rows for _, _, _, rows in layout), keep), BF16),
        [VMEM] * len(arrays) + [ANY],
        (*arrays, dep),
        out_specs=VMEM,
    )


DIRECT, SQUARE = "direct", "square"


def weight_kernel(n_half, n_row, layout, when, form, count, cot_ref, cot_other_ref, other_ref, *refs):
    arrays, own_ref, send_refs = refs[:count], refs[count + 1], refs[count + 2 : -2]
    mine_ref, total_ref = refs[-2:]
    dp, row = lax.axis_index("dp"), lax.axis_index("row")
    sub = own_ref.shape[0]
    apart = (2,) if form == SQUARE else ()

    def body():
        copy_half(dp, n_half, split_lines(arrays, len(layout)), layout, mine_ref)
        base = start = 0
        for _, size, _, rows in layout:

            @pl.loop(0, n_row)
            def _(step):
                at = span(base + (row ^ step) * size, size)
                value = dot(mine_ref[at, :], cot_ref[...], 1, 1) + dot(other_ref[at, :], cot_other_ref[...], 1, 1)
                target = pl.ds(start, size)

                @pl.when(step == 0)
                def _():
                    own_ref[target, :] = value

                @pl.when(step > 0)
                def _():
                    total_ref[step - 1, target, :] = value

            start += size
            base += n_half * rows
        bound = tile_max(total_ref[0])
        for step in range(2, n_row):
            if step not in apart:
                bound = jnp.maximum(bound, tile_max(total_ref[step - 1]))
        for step in apart:
            send_refs[1][...] = total_ref[step - 1]
        if form == SQUARE:
            expo = exponent(bound)
            scale = jnp.exp2(expo)[0:1, 0:1]
            size, count = chunks(sub)
            for n, step in enumerate((1, 3)):

                @pl.loop(0, count)
                def _(i):
                    value = total_ref[step - 1, span(i * size, size), :]
                    send_refs[0][span(n * sub + i * size, size), :] = power(value, scale)

            write_header(send_refs[0], expo)
        else:
            for n, send_ref in enumerate(send_refs):
                write_payload(send_ref, lambda first, size: total_ref[n, span(first, size), :], bound)

    run_if(wanted(when, dp, n_half), body)


def weight_partial(cot, cot_other, other, lines, layout, n_half, n_row, when, form, dep):
    half, keep = other.shape
    heads = cot.shape[0]
    sub = sum(size for _, size, _, _ in layout)
    arrays = [array for line in lines for array in line]
    if form == SQUARE:
        outputs = [shape((2 * sub + HEADER, heads), BF16), shape((sub, heads), F32)]
    else:
        outputs = [shape((sub + HEADER, heads), BF16)] * (n_row - 1)
    return call(
        functools.partial(weight_kernel, n_half, n_row, layout, when, form, len(arrays)),
        "grad_weight_partial",
        [shape((sub, heads), F32)] + outputs,
        [VMEM] * (3 + len(arrays)) + [ANY],
        (cot, cot_other, other, *arrays, dep),
        scratch=[pltpu.VMEM((half, keep), BF16), pltpu.VMEM((n_row - 1, sub, heads), F32)],
        mib=24,
    )


def weight_middle_kernel(n_half, when, kept_ref, came_ref, dep_ref, out_ref):
    sub = kept_ref.shape[0]

    def body():
        undo, bound = read_header(came_ref)

        def total(first, size):
            return kept_ref[span(first, size), :] + root(came_ref[span(sub + first, size), :], undo)

        write_payload(out_ref, total, bound + tile_max(kept_ref[...]))

    run_if(wanted(when, lax.axis_index("dp"), n_half), body)


def weight_middle(kept, came, n_half, when, dep):
    sub, heads = kept.shape
    return call(
        functools.partial(weight_middle_kernel, n_half, when),
        "grad_weight_middle",
        shape((sub + HEADER, heads), BF16),
        [VMEM] * 2 + [ANY],
        (kept, came, dep),
        out_specs=VMEM,
    )


def weight_last_kernel(n_came, start, n_half, when, own_ref, *refs):
    came_refs, (out_ref, done_ref, total_ref, sem) = refs[:n_came], refs[-4:]
    sub = own_ref.shape[0]
    done_ref[...] = jnp.zeros_like(done_ref)

    def body():
        undo = [read_header(came)[0] for came in came_refs]
        size = 16
        steps = sub // size
        copies = []
        for first, last in ((0, steps // 2), (steps // 2, steps)):

            @pl.loop(first, last)
            def _(i):
                rows = span(i * size, size)
                total = own_ref[rows, :]
                for came, scale in zip(came_refs, undo):
                    total = total + root(came[rows, :], scale)
                total_ref[rows, :] = total

            rows = pl.ds(first * size, (last - first) * size)
            target = out_ref.at[pl.ds(start + first * size, (last - first) * size), :]
            copies.append(pltpu.make_async_copy(total_ref.at[rows, :], target, sem.at[len(copies)]))
            copies[-1].start()
        for copy in copies:
            copy.wait()

    run_if(wanted(when, lax.axis_index("dp"), n_half), body)


def weight_last(own, came, base, dep, start, w_rows, n_half, when):
    sub, heads = own.shape
    again = base.shape == (w_rows, heads) and base.dtype == F32
    return call(
        functools.partial(weight_last_kernel, len(came), start, n_half, when),
        "grad_weight_last",
        [shape((w_rows, heads), F32), TOKEN],
        [VMEM] * (1 + len(came)) + [HBM if again else ANY, ANY],
        (own, *came, base, dep),
        out_specs=[HBM, VMEM],
        scratch=[pltpu.VMEM((sub, heads), F32), pltpu.SemaphoreType.DMA((2,))],
        aliases={1 + len(came): 0} if again else None,
    )


def query_kernel(sizes, blocks, n_half, *refs):
    parts = len(sizes)
    w_refs = refs[: 2 * parts]
    out_ref, done_ref, tile_ref, sem, *panels = refs[-4 - parts :]
    done_ref[...] = jnp.zeros_like(done_ref)
    pieces = refs[2 * parts : -5 - parts]
    middle, outer = pieces[:3], pieces[3:]
    per_part = len(outer) // parts
    dp = lax.axis_index("dp")
    for p, (_, _, offset, rows) in enumerate(part_rows(sizes, blocks)):
        mine = outer[p * per_part : (p + 1) * per_part]
        line = mine[: per_part // 2] + middle + mine[per_part // 2 :]
        for came, shard, ref in each_shard(line, offset, rows):

            @pl.when(came)
            def _():
                place = (shard // n_half ^ dp) * n_half + shard % n_half
                panels[p][span(place * rows, rows), :] = ref[...]

    tile = tile_ref.shape[1]

    def copy(i):
        return pltpu.make_async_copy(tile_ref.at[i], out_ref.at[span(i * tile, tile), :], sem.at[i])

    count = out_ref.shape[0] // tile

    @pl.loop(0, count)
    def _(i):
        heads = pl.ds(pl.multiple_of(i * tile, tile), tile)
        total = jnp.zeros(tile_ref.shape[1:], F32)
        for p in range(parts):
            for n in range(2):
                w_ref = w_refs[2 * p + n]
                half = w_ref.shape[0]
                total = total + dot(w_ref[:, heads], panels[p][pl.ds(n * half, half), :], 0, 0)
        tile_ref[i] = total.astype(BF16)
        copy(i).start()

    for i in range(count):
        copy(i).wait()


def all_queries(w_halves, lines, sizes, blocks, n_half, dep):
    heads = w_halves[0].shape[1]
    keep = lines[0][0].shape[1]
    middle = len(lines[0]) // 2
    pieces = lines[0][middle - 1 : middle + 2]
    for line in lines:
        pieces = pieces + line[: middle - 1] + line[middle + 2 :]
    tile = 256
    return call(
        functools.partial(query_kernel, sizes, blocks, n_half),
        "queries",
        [shape((heads, keep), BF16), TOKEN],
        [VMEM] * (len(w_halves) + len(pieces)) + [ANY],
        (*w_halves, *pieces, dep),
        out_specs=[HBM, VMEM],
        scratch=[pltpu.VMEM((heads // tile, tile, keep), BF16), pltpu.SemaphoreType.DMA((heads // tile,))]
        + [pltpu.VMEM((2 * w.shape[0], keep), BF16) for w in w_halves[::2]],
        mib=20,
    )


def per_device(tokens, kept_index, w_query, cotangent):
    n_dp, n_row, n_col = (lax.axis_size(a) for a in ("dp", "row", "col"))
    seq_x = tokens[0]
    cot = cotangent[0]
    d_dev, seq_dev = seq_x.shape
    w_rows, heads = w_query.shape
    keep_dev = cot.shape[1]
    drift = keep_dev // 4
    sizes = part_sizes(w_rows)
    parts = len(sizes)
    blocks = d_dev // w_rows
    n_half = n_col // n_dp
    layout = list(part_rows(sizes, blocks))

    def to_row(value, step):
        return lax.ppermute(value, "row", [(r, r ^ step) for r in range(n_row)])

    def to_core(value):
        return lax.ppermute(value, "dp", [(i, i ^ 1) for i in range(n_dp)])

    def along(value, sources, step):
        return lax.ppermute(value, "col", [(c, c + step) for c in sources])

    if parts == 2 and n_row == 4:
        own_w = call(
            functools.partial(split_kernel, sizes),
            "split_rows",
            [shape((size, heads), BF16) for size in sizes],
            [HBM],
            (w_query,),
            scratch=[pltpu.SemaphoreType.DMA((parts,))],
        )
        ways = ((1, 2), (2, 1))
        pieces = join([(w, to_row(w, one)) for w, (one, _) in zip(own_w, ways)])
        pieces = [*pieces] + [to_row(pair, two) for pair, (_, two) in zip(pieces, ways)]
        plan = [
            ((0, p, 0), (one, p, size), (two, p + 2, 0), (3, p + 2, size))
            for p, ((one, two), size) in enumerate(zip(ways, sizes))
        ]
    else:
        pieces = [w_query] + [to_row(w_query, step) for step in range(1, n_row)]
        plan = [tuple((step, step, start) for step in range(n_row)) for start, _, _, _ in layout]

    leaving, rows = call(
        functools.partial(pick_leaving_kernel, blocks, sizes, n_row, keep_dev),
        "pick_leaving",
        [shape((d_dev, drift), BF16), shape((d_dev, seq_dev), BF16)],
        [VMEM, ANY],
        (kept_index, seq_x),
        scratch=[pltpu.VMEM((seq_dev, drift), BF16), pltpu.SemaphoreType.DMA((blocks,))],
        mib=40,
    )
    arrived = lax.ppermute(leaving, "row", [(r, r + 1) for r in range(n_row - 1)])
    cot_other = to_core(cot)
    picked = call(
        functools.partial(pick_own_kernel, blocks, sizes),
        "pick_own",
        shape((d_dev, keep_dev), BF16),
        [VMEM] * 2,
        (kept_index, rows),
        out_specs=VMEM,
        scratch=[pltpu.VMEM((seq_dev, keep_dev), BF16)],
    )
    kept = call(
        add_arrived_kernel,
        "add_arrived",
        shape((d_dev, keep_dev), BF16),
        [VMEM] * 2 + [ANY],
        (arrived, picked, cot_other),
        out_specs=VMEM,
        aliases={1: 0},
    )


    right = [[along(kept, range(n_col - 1), 1)] for _ in range(parts)]
    left = [[along(kept, range(1, n_col), -1)] for _ in range(parts)]
    for p in range(1, parts):
        right[p][0], left[p][0] = right[0][0], left[0][0]
    token = kept
    def line_of(p):
        return right[p][n_col - 2 :: -1] + [kept] + left[p][: n_col - 1]

    def step(p, t):
        nonlocal token
        offset = layout[p][2] if t == 1 else 0
        out_r, out_l = line_step(
            n_col, n_half, t, offset, layout[p][3], mine[p], other[p], cot, right[p][-1], left[p][-1], token
        )
        token = out_r
        right[p].append(along(out_r, range(n_col - 1), 1))
        left[p].append(along(out_l, range(1, n_col), -1))

    def device(s, r, c):
        return (s * n_row + r) * n_col + c

    def taking(when):
        return [
            (s, c) for s in range(n_dp) for c in range(n_col) if when is None or (c // n_half == s) == when
        ]

    def give(parts_of, when, lines):
        nonlocal token
        token = other_half(lines, [layout[p] for p in parts_of], n_half, when, token)
        pairs = [((1 - s) * n_col + c, s * n_col + c) for s, c in taking(when)]
        return lax.ppermute(token, ("dp", "col"), pairs)

    def to_rows(send, step, when):
        pairs = [(device(s, r, c), device(s, r ^ step, c)) for s, c in taking(when) for r in range(n_row)]
        return lax.ppermute(send, ("dp", "row", "col"), pairs)

    def weigh(parts_of, when, lines, theirs, form):
        nonlocal token
        own, *sends = weight_partial(
            cot, cot_other, theirs, lines, [layout[p] for p in parts_of], n_half, n_row, when, form, token
        )
        token = own
        return own, sends, layout[parts_of[0]][0], when

    def send_first(own, sends, start, when):
        return own, [to_rows(sends[0], 1, when), sends[1]], start, when

    def send_all(own, sends, start, when):
        return own, [to_rows(send, step, when) for step, send in enumerate(sends, 1)], start, when

    def second(own, came, start, when):
        nonlocal token
        token = weight_middle(came[1], came[0], n_half, when, token)
        return own, [came[0], to_rows(token, 2, when)], start, when

    grad_kept, grad_weight = leaving, leaving

    def finish_kept(p):
        nonlocal grad_kept, token
        start, size = layout[p][:2]
        grad_kept, token = last_sums(
            mine[p], other[p], cot, right[p][-1], left[p][-1], grad_kept, token, start, size, blocks, n_half, d_dev
        )

    def finish_weight(own, came, start, when):
        nonlocal grad_weight, token
        grad_weight, token = weight_last(own, came, grad_weight, token, start, w_rows, n_half, when)

    def collect_all():
        nonlocal token
        shares = collect(pieces, plan, sizes, [token, right[0][0], left[0][0]])
        token = shares[0]
        return shares, [to_core(share) for share in shares]

    def ask():
        nonlocal token
        halves = [h for p in range(parts) for h in (mine[p], other[p])]
        queries, token = all_queries(halves, [line_of(p) for p in range(parts)], sizes, blocks, n_half, token)
        return queries

    every = tuple(range(parts))
    if parts == 2 and n_half == 2 and n_row == 4:
        whole = [right[0][0], kept, left[0][0]]
        theirs = give(every, True, [whole, whole])
        mine, other = collect_all()
        step(0, 1)
        step(1, 1)
        first = send_first(*weigh(every, True, [whole, whole], theirs, SQUARE))
        step(0, 2)
        step(1, 2)
        step(0, 3)
        step(1, 3)
        finish_kept(0)
        theirs = give(every, False, [line_of(p) for p in every])
        first = second(*first)
        late = send_all(*weigh(every, False, [line_of(p) for p in every], theirs, DIRECT))
        finish_weight(*first)
        queries = ask()
        finish_kept(1)
        finish_weight(*late)
    else:
        mine, other = collect_all()
        for t in range(1, n_col):
            for p in every:
                step(p, t)
        theirs = give(every, None, [line_of(p) for p in every])
        late = send_all(*weigh(every, None, [line_of(p) for p in every], theirs, DIRECT))
        queries = ask()
        for p in every:
            finish_kept(p)
        finish_weight(*late)
    return (queries[None], grad_kept[None], grad_weight)


def part_sizes(w_rows):
    return (w_rows // 2, w_rows // 2) if w_rows % 32 == 0 else (w_rows,)


def solution(mesh):
    in_specs = (
        P("dp", "col", "row"),
        P("dp", None),
        P(("dp", "row"), "col"),
        P("dp", "col", "row"),
    )
    out_specs = (P("dp", "col", "row"), P("dp", "col", "row"), P(("dp", "row"), "col"))
    return jax.shard_map(
        per_device, mesh=mesh, in_specs=in_specs, out_specs=out_specs, check_vma=False
    )
```

```python
import functools

import jax
import jax.numpy as jnp
from jax import lax
from jax.experimental import pallas as pl
from jax.experimental.pallas import tpu as pltpu
from jax.sharding import PartitionSpec as P

HEADER = 16
OFFSET = 128.0
F32 = jnp.float32
BF16 = jnp.bfloat16
ANY = pl.BlockSpec(memory_space=pl.ANY)
VMEM = pl.BlockSpec(memory_space=pltpu.VMEM)
HBM = pl.BlockSpec(memory_space=pltpu.HBM)


def call(kernel, name, out_shape, in_specs, args, out_specs=None, scratch=(), aliases=None, flops=0, mib=14):
    moved = sum(a.size * a.dtype.itemsize for a, s in zip(args, in_specs) if s is VMEM)
    return pl.pallas_call(
        kernel,
        out_shape=out_shape,
        in_specs=in_specs,
        out_specs=out_specs if out_specs is not None else [VMEM] * len(out_shape),
        scratch_shapes=scratch,
        input_output_aliases=aliases or {},
        compiler_params=pltpu.CompilerParams(vmem_limit_bytes=mib * 2**20),
        cost_estimate=pl.CostEstimate(flops=1, bytes_accessed=1, transcendentals=0),
        name=name,
    )(*args)


def shape(dims, dtype):
    return jax.ShapeDtypeStruct(dims, dtype)


TOKEN = shape((8, 128), F32)


def dot(a, b, ca, cb):
    return lax.dot_general(a, b, (((ca,), (cb,)), ((), ())), preferred_element_type=F32)


def span(start, size):
    return pl.ds(pl.multiple_of(start, 16), size)


def chunks(rows):
    size = 32 if rows % 32 == 0 else 16
    return size, rows // size


def exponent(bound):
    return jnp.clip(jnp.floor(14.99 - jnp.log2(jnp.maximum(bound, 1e-30))), -100.0, 100.0)


def power(values, scale):
    v = values * scale
    square = v * v
    fourth = square * square
    return (fourth * square * (v * jnp.abs(v))).astype(BF16)


def root(code, scale):
    y = code.astype(F32)
    quarter = lax.rsqrt(lax.rsqrt(jnp.maximum(jnp.abs(y), 1e-37)))
    size = quarter * lax.rsqrt(quarter) * scale
    return jnp.where(y > 0.0, size, jnp.where(y < 0.0, -size, 0.0))


def tile_max(values):
    most = jnp.max(jnp.abs(values), axis=0, keepdims=True)
    return jnp.broadcast_to(jnp.max(most, axis=1, keepdims=True), (8, 128))


def write_header(out_ref, expo):
    rows = out_ref.shape[0] - HEADER
    code = jnp.broadcast_to((expo + OFFSET)[0:1, 0:1], (HEADER, out_ref.shape[1]))
    out_ref[rows:, :] = code.astype(BF16)


def write_payload(out_ref, value_of, bound):
    expo = exponent(bound)
    scale = jnp.exp2(expo)[0:1, 0:1]
    size, count = chunks(out_ref.shape[0] - HEADER)

    @pl.loop(0, count)
    def _(i):
        out_ref[span(i * size, size), :] = power(value_of(i * size, size), scale)

    write_header(out_ref, expo)


def read_header(came_ref):
    rows = came_ref.shape[0] - HEADER
    code = came_ref[rows:, :][0:8, 0:128].astype(F32)
    came = code > 0.0
    expo = jnp.where(came, code - OFFSET, 0.0)
    return jnp.exp2(-expo)[0:1, 0:1], jnp.where(came, jnp.exp2(15.0 - expo), 0.0)


def part_rows(sizes, blocks):
    start = 0
    for size in sizes:
        yield start, size, start * blocks, size * blocks
        start += size


def onehot_of(index_ref, first, count, seq_dev):
    index = index_ref[:, pl.ds(pl.multiple_of(first, 128), count)] - lax.axis_index("row") * seq_dev
    positions = lax.broadcasted_iota(jnp.int32, (seq_dev, count), 0)
    return (positions == index).astype(F32).astype(BF16)


def pick_leaving_kernel(blocks, sizes, n_row, keep_dev, index_ref, x_ref, leaving_ref, rows_ref, onehot_ref, sem):
    d_dev, seq_dev = rows_ref.shape
    step = d_dev // blocks

    def copy(b):
        rows = pl.ds(b * step, step)
        return pltpu.make_async_copy(x_ref.at[rows, :], rows_ref.at[rows, :], sem.at[b])

    for b in range(blocks):
        copy(b).start()
    after = jnp.minimum(lax.axis_index("row") + 1, n_row - 1) * keep_dev
    onehot_ref[...] = onehot_of(index_ref, after, leaving_ref.shape[1], seq_dev)
    for b in range(blocks):
        copy(b).wait()
        for start, size, offset, _ in part_rows(sizes, blocks):
            picked = dot(rows_ref[pl.ds(b * step + start, size), :], onehot_ref[...], 1, 0)
            leaving_ref[pl.ds(offset + b * size, size), :] = picked.astype(BF16)


def pick_own_kernel(blocks, sizes, index_ref, rows_ref, kept_ref, onehot_ref):
    d_dev, seq_dev = rows_ref.shape
    keep_dev = kept_ref.shape[1]
    onehot_ref[...] = onehot_of(index_ref, lax.axis_index("row") * keep_dev, keep_dev, seq_dev)
    for b in range(blocks):
        for start, size, offset, _ in part_rows(sizes, blocks):
            picked = dot(rows_ref[pl.ds(b * (d_dev // blocks) + start, size), :], onehot_ref[...], 1, 0)
            kept_ref[pl.ds(offset + b * size, size), :] = picked.astype(BF16)


def add_arrived_kernel(arrived_ref, in_ref, dep_ref, out_ref):
    drift = arrived_ref.shape[1]
    out_ref[:, :drift] = in_ref[:, :drift] + arrived_ref[...]


def nothing_kernel(*refs):
    pass


def after(values, deps):
    return call(
        nothing_kernel,
        "after",
        [shape(v.shape, v.dtype) for v in values],
        [ANY] * (len(values) + len(deps)),
        (*values, *deps),
        out_specs=[ANY] * len(values),
        aliases={i: i for i in range(len(values))},
        mib=1,
    )


def split_kernel(sizes, w_ref, *refs):
    out_refs, sem = refs[:-1], refs[-1]
    copies = [
        pltpu.make_async_copy(w_ref.at[pl.ds(start, size), :], out_refs[p], sem.at[p])
        for p, (start, size, _, _) in enumerate(part_rows(sizes, 1))
    ]
    for copy in copies:
        copy.start()
    for copy in copies:
        copy.wait()


def join_kernel(*refs):
    count = len(refs) // 3
    for n in range(count):
        top, bottom, out_ref = refs[2 * n], refs[2 * n + 1], refs[2 * count + n]
        rows = top.shape[0]
        out_ref[:rows, :] = top[...]
        out_ref[rows:, :] = bottom[...]


def join(pairs):
    arrays = [array for pair in pairs for array in pair]
    return call(
        join_kernel,
        "join_rows",
        [shape((a.shape[0] + b.shape[0], a.shape[1]), a.dtype) for a, b in pairs],
        [VMEM] * len(arrays),
        arrays,
    )


def collect_kernel(plan, *refs):
    out_refs = refs[-len(plan) :]
    row = lax.axis_index("row")
    for out_ref, sources in zip(out_refs, plan):
        size = out_ref.shape[0] // len(sources)
        for step, piece, first in sources:
            out_ref[span((row ^ step) * size, size), :] = refs[piece][pl.ds(first, size), :]


def collect(pieces, plan, sizes, deps):
    heads = pieces[0].shape[1]
    return call(
        functools.partial(collect_kernel, plan),
        "collect_rows",
        [shape((len(sources) * size, heads), BF16) for sources, size in zip(plan, sizes)],
        [VMEM] * len(pieces) + [ANY] * len(deps),
        (*pieces, *deps),
    )


def copy_rows(out_ref, from_ref, first):
    size, count = chunks(out_ref.shape[0])

    @pl.loop(0, count)
    def _(i):
        out_ref[span(i * size, size), :] = from_ref[span(first + i * size, size), :]


def partial_into(out_ref, block, n_half, mine_ref, other_ref, cot_ref, rows_ref):
    shard = out_ref.shape[0]
    first = (block % n_half) * shard
    here = block // n_half == lax.axis_index("dp")
    pl.when(here)(lambda: copy_rows(rows_ref, mine_ref, first))
    pl.when(jnp.logical_not(here))(lambda: copy_rows(rows_ref, other_ref, first))
    out_ref[...] = dot(rows_ref[...], cot_ref[...], 1, 0)


def step_kernel(
    n_col, n_half, t, offset, mine_ref, other_ref, cot_ref, came_r, came_l, dep_ref, out_r, out_l, term_ref, rows_ref
):
    shard = out_r.shape[0] - HEADER
    col = lax.axis_index("col")

    @pl.loop(0, 2)
    def _(way):
        place = jnp.where(way == 0, col, n_col - 1 - col)

        @pl.when(place < t)
        def _():
            block = jnp.where(way == 0, n_col - t + col, t - n_col + col)
            partial_into(term_ref.at[way], block, n_half, mine_ref, other_ref, cot_ref, rows_ref)

    for way, (place, came, out) in enumerate(((col, came_r, out_r), (n_col - 1 - col, came_l, out_l))):
        pl.when(place >= t)(lambda: copy_rows(out.at[pl.ds(0, shard), :], came, offset))

        @pl.when(place < t)
        def _():
            bound = tile_max(term_ref[way])
            if t == 1:
                write_payload(out, lambda first, size: term_ref[way, span(first, size), :], bound)
            else:
                undo, came_bound = read_header(came)

                def total(first, size):
                    rows = span(first, size)
                    return term_ref[way, rows, :] + root(came[rows, :], undo)

                write_payload(out, total, bound + came_bound)


def line_step(n_col, n_half, t, offset, shard, mine, other, cot, came_r, came_l, dep):
    keep = cot.shape[1]
    payload = shape((shard + HEADER, keep), BF16)
    return call(
        functools.partial(step_kernel, n_col, n_half, t, offset),
        "line_step",
        [payload, payload],
        [VMEM] * 5 + [ANY],
        (mine, other, cot, came_r, came_l, dep),
        scratch=[pltpu.VMEM((2, shard, keep), F32), pltpu.VMEM((shard, cot.shape[0]), BF16)],
    )


def last_kernel(
    start, size, blocks, n_half, mine_ref, other_ref, cot_ref, r_ref, l_ref, base_ref, dep_ref, out_ref, *rest
):
    done_ref, total_ref, rows_ref, sem = rest
    done_ref[...] = jnp.zeros_like(done_ref)
    step = out_ref.shape[0] // blocks
    partial_into(total_ref, lax.axis_index("col"), n_half, mine_ref, other_ref, cot_ref, rows_ref)
    undo_r, _ = read_header(r_ref)
    undo_l, _ = read_header(l_ref)
    few, count = chunks(size)
    copies = []
    for b in range(blocks):

        @pl.loop(0, count)
        def _(i):
            rows = span(b * size + i * few, few)
            came = root(r_ref[rows, :], undo_r) + root(l_ref[rows, :], undo_l)
            total_ref[rows, :] = total_ref[rows, :] + came

        target = out_ref.at[pl.ds(b * step + start, size), :]
        copies.append(pltpu.make_async_copy(total_ref.at[pl.ds(b * size, size), :], target, sem.at[b]))
        copies[-1].start()
    for copy in copies:
        copy.wait()


def last_sums(mine, other, cot, came_r, came_l, base, dep, start, size, blocks, n_half, d_dev):
    shard, keep = came_r.shape[0] - HEADER, came_r.shape[1]
    return call(
        functools.partial(last_kernel, start, size, blocks, n_half),
        "grad_kept_last",
        [shape((d_dev, keep), F32), TOKEN],
        [VMEM] * 5 + [HBM if start else ANY, ANY],
        (mine, other, cot, came_r, came_l, base, dep),
        out_specs=[HBM, VMEM],
        scratch=[
            pltpu.VMEM((shard, keep), F32),
            pltpu.VMEM((shard, cot.shape[0]), BF16),
            pltpu.SemaphoreType.DMA((blocks,)),
        ],
        aliases={5: 0} if start else None,
    )


def each_shard(line, offset, rows):
    n_col = lax.axis_size("col")
    col = lax.axis_index("col")
    for n, ref in enumerate(line):
        away = n - len(line) // 2
        shard = col + away
        whole = abs(away) < 2
        yield (shard >= 0) & (shard < n_col), shard, ref.at[pl.ds(offset if whole else 0, rows), :]


def early(dp, n_half):
    return lax.axis_index("col") // n_half == dp


def wanted(when, dp, n_half):
    return None if when is None else early(dp, n_half) == when


def run_if(condition, body):
    if condition is None:
        body()
    else:
        pl.when(condition)(body)


def copy_half(dp, n_half, lines, layout, out_ref):
    base = 0
    for line, (_, _, offset, rows) in zip(lines, layout):
        for came, shard, ref in each_shard(line, offset, rows):

            @pl.when(came & (shard // n_half == dp))
            def _():
                out_ref[span(base + (shard % n_half) * rows, rows), :] = ref[...]

        base += n_half * rows


def half_kernel(n_half, layout, when, *refs):
    arrays, out_ref = refs[:-2], refs[-1]
    other = 1 - lax.axis_index("dp")
    run_if(
        wanted(when, other, n_half),
        lambda: copy_half(other, n_half, split_lines(arrays, len(layout)), layout, out_ref),
    )


def split_lines(arrays, parts):
    count = len(arrays) // parts
    return [arrays[p * count : (p + 1) * count] for p in range(parts)]


def other_half(lines, layout, n_half, when, dep):
    keep = lines[0][0].shape[1]
    arrays = [array for line in lines for array in line]
    return call(
        functools.partial(half_kernel, n_half, layout, when),
        "half_for_other_core",
        shape((n_half * sum(rows for _, _, _, rows in layout), keep), BF16),
        [VMEM] * len(arrays) + [ANY],
        (*arrays, dep),
        out_specs=VMEM,
    )


DIRECT, SQUARE = "direct", "square"


def weight_kernel(n_half, n_row, layout, when, form, count, cot_ref, cot_other_ref, other_ref, *refs):
    arrays, own_ref, send_refs = refs[:count], refs[count + 1], refs[count + 2 : -2]
    mine_ref, total_ref = refs[-2:]
    dp, row = lax.axis_index("dp"), lax.axis_index("row")
    sub = own_ref.shape[0]
    apart = (2,) if form == SQUARE else ()

    def body():
        copy_half(dp, n_half, split_lines(arrays, len(layout)), layout, mine_ref)
        base = start = 0
        for _, size, _, rows in layout:

            @pl.loop(0, n_row)
            def _(step):
                at = span(base + (row ^ step) * size, size)
                value = dot(mine_ref[at, :], cot_ref[...], 1, 1) + dot(other_ref[at, :], cot_other_ref[...], 1, 1)
                target = pl.ds(start, size)

                @pl.when(step == 0)
                def _():
                    own_ref[target, :] = value

                @pl.when(step > 0)
                def _():
                    total_ref[step - 1, target, :] = value

            start += size
            base += n_half * rows
        bound = tile_max(total_ref[0])
        for step in range(2, n_row):
            if step not in apart:
                bound = jnp.maximum(bound, tile_max(total_ref[step - 1]))
        for step in apart:
            send_refs[1][...] = total_ref[step - 1]
        if form == SQUARE:
            expo = exponent(bound)
            scale = jnp.exp2(expo)[0:1, 0:1]
            size, count = chunks(sub)
            for n, step in enumerate((1, 3)):

                @pl.loop(0, count)
                def _(i):
                    value = total_ref[step - 1, span(i * size, size), :]
                    send_refs[0][span(n * sub + i * size, size), :] = power(value, scale)

            write_header(send_refs[0], expo)
        else:
            for n, send_ref in enumerate(send_refs):
                write_payload(send_ref, lambda first, size: total_ref[n, span(first, size), :], bound)

    run_if(wanted(when, dp, n_half), body)


def weight_partial(cot, cot_other, other, lines, layout, n_half, n_row, when, form, dep):
    half, keep = other.shape
    heads = cot.shape[0]
    sub = sum(size for _, size, _, _ in layout)
    arrays = [array for line in lines for array in line]
    if form == SQUARE:
        outputs = [shape((2 * sub + HEADER, heads), BF16), shape((sub, heads), F32)]
    else:
        outputs = [shape((sub + HEADER, heads), BF16)] * (n_row - 1)
    return call(
        functools.partial(weight_kernel, n_half, n_row, layout, when, form, len(arrays)),
        "grad_weight_partial",
        [shape((sub, heads), F32)] + outputs,
        [VMEM] * (3 + len(arrays)) + [ANY],
        (cot, cot_other, other, *arrays, dep),
        scratch=[pltpu.VMEM((half, keep), BF16), pltpu.VMEM((n_row - 1, sub, heads), F32)],
        mib=24,
    )


def weight_middle_kernel(n_half, when, kept_ref, came_ref, dep_ref, out_ref):
    sub = kept_ref.shape[0]

    def body():
        undo, bound = read_header(came_ref)

        def total(first, size):
            return kept_ref[span(first, size), :] + root(came_ref[span(sub + first, size), :], undo)

        write_payload(out_ref, total, bound + tile_max(kept_ref[...]))

    run_if(wanted(when, lax.axis_index("dp"), n_half), body)


def weight_middle(kept, came, n_half, when, dep):
    sub, heads = kept.shape
    return call(
        functools.partial(weight_middle_kernel, n_half, when),
        "grad_weight_middle",
        shape((sub + HEADER, heads), BF16),
        [VMEM] * 2 + [ANY],
        (kept, came, dep),
        out_specs=VMEM,
    )


def weight_last_kernel(n_came, start, n_half, when, own_ref, *refs):
    came_refs, (out_ref, done_ref, total_ref, sem) = refs[:n_came], refs[-4:]
    sub = own_ref.shape[0]
    done_ref[...] = jnp.zeros_like(done_ref)

    def body():
        undo = [read_header(came)[0] for came in came_refs]
        size = 16
        steps = sub // size
        copies = []
        for first, last in ((0, steps // 2), (steps // 2, steps)):

            @pl.loop(first, last)
            def _(i):
                rows = span(i * size, size)
                total = own_ref[rows, :]
                for came, scale in zip(came_refs, undo):
                    total = total + root(came[rows, :], scale)
                total_ref[rows, :] = total

            rows = pl.ds(first * size, (last - first) * size)
            target = out_ref.at[pl.ds(start + first * size, (last - first) * size), :]
            copies.append(pltpu.make_async_copy(total_ref.at[rows, :], target, sem.at[len(copies)]))
            copies[-1].start()
        for copy in copies:
            copy.wait()

    run_if(wanted(when, lax.axis_index("dp"), n_half), body)


def weight_last(own, came, base, dep, start, w_rows, n_half, when):
    sub, heads = own.shape
    again = base.shape == (w_rows, heads) and base.dtype == F32
    return call(
        functools.partial(weight_last_kernel, len(came), start, n_half, when),
        "grad_weight_last",
        [shape((w_rows, heads), F32), TOKEN],
        [VMEM] * (1 + len(came)) + [HBM if again else ANY, ANY],
        (own, *came, base, dep),
        out_specs=[HBM, VMEM],
        scratch=[pltpu.VMEM((sub, heads), F32), pltpu.SemaphoreType.DMA((2,))],
        aliases={1 + len(came): 0} if again else None,
    )


def query_kernel(sizes, blocks, n_half, *refs):
    parts = len(sizes)
    w_refs = refs[: 2 * parts]
    out_ref, done_ref, tile_ref, sem, *panels = refs[-4 - parts :]
    done_ref[...] = jnp.zeros_like(done_ref)
    pieces = refs[2 * parts : -5 - parts]
    middle, outer = pieces[:3], pieces[3:]
    per_part = len(outer) // parts
    dp = lax.axis_index("dp")
    for p, (_, _, offset, rows) in enumerate(part_rows(sizes, blocks)):
        mine = outer[p * per_part : (p + 1) * per_part]
        line = mine[: per_part // 2] + middle + mine[per_part // 2 :]
        for came, shard, ref in each_shard(line, offset, rows):

            @pl.when(came)
            def _():
                place = (shard // n_half ^ dp) * n_half + shard % n_half
                panels[p][span(place * rows, rows), :] = ref[...]

    tile = tile_ref.shape[1]

    def copy(i):
        return pltpu.make_async_copy(tile_ref.at[i], out_ref.at[span(i * tile, tile), :], sem.at[i])

    count = out_ref.shape[0] // tile

    @pl.loop(0, count)
    def _(i):
        heads = pl.ds(pl.multiple_of(i * tile, tile), tile)
        total = jnp.zeros(tile_ref.shape[1:], F32)
        for p in range(parts):
            for n in range(2):
                w_ref = w_refs[2 * p + n]
                half = w_ref.shape[0]
                total = total + dot(w_ref[:, heads], panels[p][pl.ds(n * half, half), :], 0, 0)
        tile_ref[i] = total.astype(BF16)
        copy(i).start()

    for i in range(count):
        copy(i).wait()


def all_queries(w_halves, lines, sizes, blocks, n_half, dep):
    heads = w_halves[0].shape[1]
    keep = lines[0][0].shape[1]
    middle = len(lines[0]) // 2
    pieces = lines[0][middle - 1 : middle + 2]
    for line in lines:
        pieces = pieces + line[: middle - 1] + line[middle + 2 :]
    tile = 256
    return call(
        functools.partial(query_kernel, sizes, blocks, n_half),
        "queries",
        [shape((heads, keep), BF16), TOKEN],
        [VMEM] * (len(w_halves) + len(pieces)) + [ANY],
        (*w_halves, *pieces, dep),
        out_specs=[HBM, VMEM],
        scratch=[pltpu.VMEM((heads // tile, tile, keep), BF16), pltpu.SemaphoreType.DMA((heads // tile,))]
        + [pltpu.VMEM((2 * w.shape[0], keep), BF16) for w in w_halves[::2]],
        mib=20,
    )


def per_device(tokens, kept_index, w_query, cotangent):
    n_dp, n_row, n_col = (lax.axis_size(a) for a in ("dp", "row", "col"))
    seq_x = tokens[0]
    cot = cotangent[0]
    d_dev, seq_dev = seq_x.shape
    w_rows, heads = w_query.shape
    keep_dev = cot.shape[1]
    drift = keep_dev // 4
    sizes = part_sizes(w_rows)
    parts = len(sizes)
    blocks = d_dev // w_rows
    n_half = n_col // n_dp
    layout = list(part_rows(sizes, blocks))

    def to_row(value, step):
        return lax.ppermute(value, "row", [(r, r ^ step) for r in range(n_row)])

    def to_core(value):
        return lax.ppermute(value, "dp", [(i, i ^ 1) for i in range(n_dp)])

    def along(value, sources, step):
        return lax.ppermute(value, "col", [(c, c + step) for c in sources])

    if parts == 2 and n_row == 4:
        own_w = call(
            functools.partial(split_kernel, sizes),
            "split_rows",
            [shape((size, heads), BF16) for size in sizes],
            [HBM],
            (w_query,),
            scratch=[pltpu.SemaphoreType.DMA((parts,))],
        )
        ways = ((1, 2), (2, 1))
        pieces = join([(w, to_row(w, one)) for w, (one, _) in zip(own_w, ways)])
        pieces = [*pieces] + [to_row(pair, two) for pair, (_, two) in zip(pieces, ways)]
        plan = [
            ((0, p, 0), (one, p, size), (two, p + 2, 0), (3, p + 2, size))
            for p, ((one, two), size) in enumerate(zip(ways, sizes))
        ]
    else:
        pieces = [w_query] + [to_row(w_query, step) for step in range(1, n_row)]
        plan = [tuple((step, step, start) for step in range(n_row)) for start, _, _, _ in layout]

    leaving, rows = call(
        functools.partial(pick_leaving_kernel, blocks, sizes, n_row, keep_dev),
        "pick_leaving",
        [shape((d_dev, drift), BF16), shape((d_dev, seq_dev), BF16)],
        [VMEM, ANY],
        (kept_index, seq_x),
        scratch=[pltpu.VMEM((seq_dev, drift), BF16), pltpu.SemaphoreType.DMA((blocks,))],
        mib=40,
    )
    arrived = lax.ppermute(leaving, "row", [(r, r + 1) for r in range(n_row - 1)])
    cot_other = to_core(cot)
    picked = call(
        functools.partial(pick_own_kernel, blocks, sizes),
        "pick_own",
        shape((d_dev, keep_dev), BF16),
        [VMEM] * 2,
        (kept_index, rows),
        out_specs=VMEM,
        scratch=[pltpu.VMEM((seq_dev, keep_dev), BF16)],
    )
    kept = call(
        add_arrived_kernel,
        "add_arrived",
        shape((d_dev, keep_dev), BF16),
        [VMEM] * 2 + [ANY],
        (arrived, picked, cot_other),
        out_specs=VMEM,
        aliases={1: 0},
    )


    right = [[along(kept, range(n_col - 1), 1)] for _ in range(parts)]
    left = [[along(kept, range(1, n_col), -1)] for _ in range(parts)]
    for p in range(1, parts):
        right[p][0], left[p][0] = right[0][0], left[0][0]
    token = kept
    def line_of(p):
        return right[p][n_col - 2 :: -1] + [kept] + left[p][: n_col - 1]

    def step(p, t):
        nonlocal token
        offset = layout[p][2] if t == 1 else 0
        out_r, out_l = line_step(
            n_col, n_half, t, offset, layout[p][3], mine[p], other[p], cot, right[p][-1], left[p][-1], token
        )
        token = out_r
        right[p].append(along(out_r, range(n_col - 1), 1))
        left[p].append(along(out_l, range(1, n_col), -1))

    def device(s, r, c):
        return (s * n_row + r) * n_col + c

    def taking(when):
        return [
            (s, c) for s in range(n_dp) for c in range(n_col) if when is None or (c // n_half == s) == when
        ]

    def give(parts_of, when, lines):
        nonlocal token
        token = other_half(lines, [layout[p] for p in parts_of], n_half, when, token)
        pairs = [((1 - s) * n_col + c, s * n_col + c) for s, c in taking(when)]
        return lax.ppermute(token, ("dp", "col"), pairs)

    def to_rows(send, step, when):
        pairs = [(device(s, r, c), device(s, r ^ step, c)) for s, c in taking(when) for r in range(n_row)]
        return lax.ppermute(send, ("dp", "row", "col"), pairs)

    def weigh(parts_of, when, lines, theirs, form):
        nonlocal token
        own, *sends = weight_partial(
            cot, cot_other, theirs, lines, [layout[p] for p in parts_of], n_half, n_row, when, form, token
        )
        token = own
        return own, sends, layout[parts_of[0]][0], when

    def send_first(own, sends, start, when):
        return own, [to_rows(sends[0], 1, when), sends[1]], start, when

    def send_all(own, sends, start, when):
        return own, [to_rows(send, step, when) for step, send in enumerate(sends, 1)], start, when

    def second(own, came, start, when):
        nonlocal token
        token = weight_middle(came[1], came[0], n_half, when, token)
        return own, [came[0], to_rows(token, 2, when)], start, when

    grad_kept, grad_weight = leaving, leaving

    def finish_kept(p):
        nonlocal grad_kept, token
        start, size = layout[p][:2]
        grad_kept, token = last_sums(
            mine[p], other[p], cot, right[p][-1], left[p][-1], grad_kept, token, start, size, blocks, n_half, d_dev
        )

    def finish_weight(own, came, start, when):
        nonlocal grad_weight, token
        grad_weight, token = weight_last(own, came, grad_weight, token, start, w_rows, n_half, when)

    def collect_all():
        nonlocal token
        shares = collect(pieces, plan, sizes, [token, right[0][0], left[0][0]])
        token = shares[0]
        return shares, [to_core(share) for share in shares]

    def ask():
        nonlocal token
        halves = [h for p in range(parts) for h in (mine[p], other[p])]
        queries, token = all_queries(halves, [line_of(p) for p in range(parts)], sizes, blocks, n_half, token)
        return queries

    every = tuple(range(parts))
    if parts == 2 and n_half == 2 and n_row == 4:
        whole = [right[0][0], kept, left[0][0]]
        theirs = give(every, True, [whole, whole])
        mine, other = collect_all()
        step(0, 1)
        step(1, 1)
        first = send_first(*weigh(every, True, [whole, whole], theirs, SQUARE))
        step(0, 2)
        step(1, 2)
        step(0, 3)
        step(1, 3)
        queries = ask()
        finish_kept(0)
        theirs = give(every, False, [line_of(p) for p in every])
        first = second(*first)
        late = send_all(*weigh(every, False, [line_of(p) for p in every], theirs, DIRECT))
        finish_weight(*first)
        finish_kept(1)
        finish_weight(*late)
    else:
        mine, other = collect_all()
        for t in range(1, n_col):
            for p in every:
                step(p, t)
        theirs = give(every, None, [line_of(p) for p in every])
        late = send_all(*weigh(every, None, [line_of(p) for p in every], theirs, DIRECT))
        queries = ask()
        for p in every:
            finish_kept(p)
        finish_weight(*late)
    return (queries[None], grad_kept[None], grad_weight)


def part_sizes(w_rows):
    return (w_rows // 2, w_rows // 2) if w_rows % 32 == 0 else (w_rows,)


def solution(mesh):
    in_specs = (
        P("dp", "col", "row"),
        P("dp", None),
        P(("dp", "row"), "col"),
        P("dp", "col", "row"),
    )
    out_specs = (P("dp", "col", "row"), P("dp", "col", "row"), P(("dp", "row"), "col"))
    return jax.shard_map(
        per_device, mesh=mesh, in_specs=in_specs, out_specs=out_specs, check_vma=False
    )
```
